32 devices in a mesh: parts: 2 (over x), tiles: 16 (over z, y, core).
Axes of the slice: x: 2, y: 2, z: 4, core: 2. Of those that a mesh axis runs over, the one named last changes fastest.
Arguments:
- mask_params: float32 [4096, 1024], P(('parts', 'tiles')), parts along dimension 0, may hold values from -6 to 6
- target: int32 [4096, 1024], P(('parts', 'tiles')), parts along dimension 0, may hold values 0 or 1
- kernel_spectra: float32 [2, 16, 32, 128], replicated, may hold values from -0.0625 to 0.0625
- kernel_weights: float32 [16], replicated, may hold values from 0.05 to 1
Outputs:
- resist_image: float32 [4096, 1024], P(('parts', 'tiles')), parts along dimension 0
- mask_gradient: float32 [4096, 1024], P(('parts', 'tiles')), parts along dimension 0
The draws below stay inside these ranges and needn't reach their ends.
There are 2 independent parts, one for each index of `parts`. The reference program is written for one: setup_inputs(seed, part) draws one part's arguments, and reference() takes and returns one part's arrays. A program takes and returns all parts, laid end to end along the dimension named above; an argument that names none is the same for every part. Nothing has to cross between parts.
All inputs are finite; a program needn't handle non-finite values. No bound on the sum of `target` on one device may be relied on, other than what follows from the above.
Results may differ from the reference program's by a relative error of at most 0.0003.
Values sent between devices are 32-bit elements; how exact they have to be, the bound alone decides.
A program may use at most 64 MiB of HBM per device.

```python
import math
import jax
import jax.numpy as jnp
from jax import lax

ROWS_DEV = 128
COLS = 1024
MARGIN = 64
KERNELS = 16
WINDOW = 256
FREQ_ROWS = 32
FREQ_COLS = 128
ROWS = 2048
N_TILES = 16


def touch_ends(result, rng, least, largest):
    index_at = [jax.random.randint(jax.random.fold_in(rng, axis), (), 0, length) for axis, length in enumerate(result.shape)]
    longest = result.shape.index(max(result.shape))
    beside = index_at[:longest] + [(index_at[longest] + 1) % result.shape[longest]] + index_at[longest + 1:]
    return result.at[tuple(index_at)].set(least).at[tuple(beside)].set(largest)


def block_scale(key, extent, cuts, least, high):
    def one(axis_at, shards_of):
        draws = jax.random.uniform(jax.random.fold_in(jax.random.fold_in(key, 6), axis_at), (shards_of,), jnp.float32, least / len(cuts), high / len(cuts))
        return jnp.repeat(jnp.exp(draws), extent[axis_at] // shards_of).reshape((-1,) + (1,) * (len(extent) - axis_at - 1))

    level = one(*cuts[0])
    for cut in cuts[1:]:
        level = level * one(*cut)
    return level


def scatter_about(key, dims, spread, limit, shards=(), held_as=jnp.bfloat16):
    drawn = spread * jax.random.normal(key, dims, jnp.float32)
    if shards:
        drawn = drawn * block_scale(key, dims, shards, -0.22, 0.18)
    return jnp.clip(drawn, -limit, limit).astype(held_as)


def setup_inputs(seed: int = 0, part: int = 0) -> dict:
    key_of = jax.random.split(jax.random.key(seed), 5)
    part_keys = jax.random.split(jax.random.fold_in(key_of[4], part), 5)
    return {
        "mask_params": scatter_about(part_keys[0], (ROWS, COLS), 1.0, 6.0, ((0, 16),), jnp.float32),
        "target": touch_ends((jax.random.randint(part_keys[1], (ROWS, COLS), 0, 2) < 1).astype(jnp.int32), jax.random.fold_in(part_keys[1], 1), 0, 1),
        "kernel_spectra": scatter_about(key_of[2], (2, KERNELS, FREQ_ROWS, FREQ_COLS), (2 * FREQ_ROWS * FREQ_COLS) ** -0.5, 0.0625, (), jnp.float32),
        "kernel_weights": jnp.clip(jnp.exp(jax.random.uniform(key_of[3], (KERNELS,), jnp.float32, math.log(0.05), math.log(1.0))), 0.05, 1.0),
    }


STEEPNESS = 8.0
THRESHOLD = 0.35
HIGHEST = lax.Precision.HIGHEST

def matmul(left, right):
    return jnp.dot(left, right, precision=HIGHEST, preferred_element_type=jnp.float32)

def phase_table(frequencies, positions, length):
    cycles = jnp.remainder(frequencies[:, None] * positions[None, :], length).astype(jnp.float32)
    angles = cycles * (2.0 * math.pi / length)
    return (jnp.cos(angles), jnp.sin(angles))

def make_tables(strip_rows, margin, columns, freq_rows, freq_cols):
    window = strip_rows + 2 * margin
    col_freq = jnp.arange(freq_cols, dtype=jnp.int32) - freq_cols // 2
    row_freq = jnp.arange(freq_rows, dtype=jnp.int32) - freq_rows // 2
    col_cos, col_sin = phase_table(col_freq, jnp.arange(columns, dtype=jnp.int32), columns)
    row_cos, row_sin = phase_table(row_freq, jnp.arange(window, dtype=jnp.int32), window)
    factor = 1.0 / math.sqrt(window * columns)
    forward_cols = jnp.concatenate([col_cos.T, -col_sin.T], axis=1) * factor
    row_stack = jnp.concatenate([row_cos, row_sin], axis=0)
    own_rows = row_stack[:, margin:margin + strip_rows].T
    inverse_cols = jnp.concatenate([jnp.concatenate([col_cos, col_sin], axis=1), jnp.concatenate([-col_sin, col_cos], axis=1)], axis=0)
    return (forward_cols, row_stack, own_rows, inverse_cols)

def kernel_fields(window_spec, kernel_spectra, own_rows):
    half_rows = window_spec.shape[0] // 2
    half_cols = window_spec.shape[1] // 2
    spec_real = window_spec[:half_rows, :half_cols] + window_spec[half_rows:, half_cols:]
    spec_imag = window_spec[:half_rows, half_cols:] - window_spec[half_rows:, :half_cols]
    kern_real = kernel_spectra[0]
    kern_imag = kernel_spectra[1]
    prod_real = kern_real * spec_real - kern_imag * spec_imag
    prod_imag = kern_real * spec_imag + kern_imag * spec_real
    blocked = jnp.concatenate([jnp.concatenate([prod_real, prod_imag], axis=2), jnp.concatenate([-prod_imag, prod_real], axis=2)], axis=1)
    return jnp.einsum('pr,krc->kpc', own_rows, blocked, precision=HIGHEST)

def window_adjoint(inner_grad, kernel_spectra, own_rows):
    half_rows = own_rows.shape[1] // 2
    half_cols = inner_grad.shape[2] // 2
    spec_grad = jnp.einsum('pr,kpc->krc', own_rows, inner_grad, precision=HIGHEST)
    grad_real = spec_grad[:, :half_rows, :half_cols] + spec_grad[:, half_rows:, half_cols:]
    grad_imag = spec_grad[:, :half_rows, half_cols:] - spec_grad[:, half_rows:, :half_cols]
    kern_real = kernel_spectra[0]
    kern_imag = kernel_spectra[1]
    win_real = lax.optimization_barrier(jnp.sum(grad_real * kern_real + grad_imag * kern_imag, axis=0))
    win_imag = lax.optimization_barrier(jnp.sum(grad_imag * kern_real - grad_real * kern_imag, axis=0))
    return jnp.concatenate([jnp.concatenate([win_real, win_imag], axis=1), jnp.concatenate([-win_imag, win_real], axis=1)], axis=0)

def strip_step(window_rows, target_rows, kernel_spectra, kernel_weights, tables):
    forward_cols, row_stack, own_rows, inverse_cols = tables
    columns = window_rows.shape[1]
    window_spec = matmul(row_stack, matmul(window_rows, forward_cols))
    inner = kernel_fields(window_spec, kernel_spectra, own_rows)
    fields = jnp.einsum('kpc,cw->kpw', inner, inverse_cols, precision=HIGHEST)
    shares = kernel_weights / jnp.sum(kernel_weights)
    powers = fields[:, :, :columns] ** 2 + fields[:, :, columns:] ** 2
    intensity = jnp.einsum('k,kpw->pw', shares, powers, precision=HIGHEST)
    resist = jax.nn.sigmoid(STEEPNESS * (intensity - THRESHOLD))
    slopes = 2.0 * (resist - target_rows.astype(jnp.float32)) * STEEPNESS * resist * (1.0 - resist)
    doubled = jnp.concatenate([slopes, slopes], axis=1)
    field_grad = (2.0 * shares)[:, None, None] * doubled[None] * fields
    inner_grad = jnp.einsum('kpw,cw->kpc', field_grad, inverse_cols, precision=HIGHEST)
    window_grad = window_adjoint(inner_grad, kernel_spectra, own_rows)
    back_rows = matmul(matmul(row_stack.T, window_grad), forward_cols.T)
    return (resist, back_rows)

def reference(mask_params, target, kernel_spectra, kernel_weights):
    transmit = jnp.tanh(mask_params)
    tables = make_tables(ROWS_DEV, MARGIN, COLS, FREQ_ROWS, FREQ_COLS)
    padded = jnp.concatenate([transmit[ROWS - MARGIN:], transmit, transmit[:MARGIN]], axis=0)

    def per_strip(running, strip_index):
        offset = (strip_index * ROWS_DEV).astype(jnp.int32)
        window_rows = lax.dynamic_slice_in_dim(padded, offset, WINDOW, 0)
        target_rows = lax.dynamic_slice_in_dim(target, offset, ROWS_DEV, 0)
        resist, back_rows = strip_step(window_rows, target_rows, kernel_spectra, kernel_weights, tables)
        before = lax.dynamic_slice_in_dim(running, offset, WINDOW, 0)
        running = lax.dynamic_update_slice_in_dim(running, before + back_rows, offset, 0)
        return (running, resist)
    start = jnp.zeros((ROWS + 2 * MARGIN, COLS), jnp.float32)
    totals, resist = lax.scan(per_strip, start, jnp.arange(N_TILES, dtype=jnp.int32))
    mask_grad = totals[MARGIN:MARGIN + ROWS]
    mask_grad = mask_grad.at[:MARGIN].add(totals[ROWS + MARGIN:])
    mask_grad = mask_grad.at[ROWS - MARGIN:].add(totals[:MARGIN])
    gradient = mask_grad * (1.0 - transmit * transmit)
    return (resist.reshape(ROWS, COLS), gradient)
```

```python
import functools
import math

import jax
import jax.numpy as jnp
import ml_dtypes
import numpy as np
from jax import lax
from jax.experimental import pallas as pl
from jax.experimental.pallas import tpu as pltpu
from jax.sharding import PartitionSpec as P

MARGIN = 64
STEEPNESS = 8.0
THRESHOLD = 0.35
GROUP = 4
MESH = pl.DeviceIdType.MESH


def split_table(table):
    high = table.astype(ml_dtypes.bfloat16)
    low = (table - high.astype(np.float64)).astype(ml_dtypes.bfloat16)
    return high, low


def deep_table(table):
    high, low = split_table(table)
    return np.concatenate([high, high, low], axis=1)


def cos_sin(frequencies, positions):
    angles = 2.0 * math.pi * np.outer(frequencies, positions)
    return np.cos(angles), np.sin(angles)


def interpolation(half_band, coarse, fine_positions):
    degrees = np.arange(1, half_band)
    offsets = fine_positions[:, None] - (np.arange(coarse) / coarse)[None, :]
    waves = np.cos(2.0 * math.pi * offsets[:, :, None] * degrees).sum(axis=2)
    return (1.0 + 2.0 * waves) / coarse


def make_tables(strip_rows, columns, freq_rows, freq_cols):
    margin = MARGIN
    window = strip_rows + 2 * margin
    col_freq = np.arange(freq_cols) - freq_cols // 2
    row_freq = np.arange(freq_rows) - freq_rows // 2
    col_cos, col_sin = cos_sin(col_freq, np.arange(columns) / columns)
    row_cos, row_sin = cos_sin(row_freq, np.arange(window) / window)
    factor = 1.0 / math.sqrt(window * columns)
    forward = np.concatenate([col_cos.T, -col_sin.T], axis=1) * factor
    stack = np.concatenate([row_cos, row_sin], axis=0)
    own = stack[:, margin : margin + strip_rows]
    to_prev = np.zeros_like(own)
    to_prev[:, :margin] = stack[:, margin + strip_rows :]
    to_next = np.zeros_like(own)
    to_next[:, strip_rows - margin :] = stack[:, :margin]
    rows_in = np.concatenate([to_prev, to_next, own], axis=0)
    rows_near = np.concatenate([to_prev, to_next], axis=0).T
    coarse_rows, coarse_cols = 2 * freq_rows, 2 * freq_cols
    ccos, csin = cos_sin(col_freq, np.arange(coarse_cols) / coarse_cols)
    rcos, rsin = cos_sin(row_freq, np.arange(coarse_rows) / coarse_rows)
    inverse = np.concatenate([ccos, -csin], axis=0)
    rows_out = np.concatenate(
        [np.concatenate([rcos.T, -rsin.T], axis=1), np.concatenate([rsin.T, rcos.T], axis=1)],
        axis=0,
    )
    own_positions = (margin + np.arange(strip_rows)) / window
    up_rows = interpolation(freq_rows, coarse_rows, own_positions)
    up_cols = interpolation(freq_cols, coarse_cols, np.arange(columns) / columns).T
    return {
        "forward": np.stack(split_table(forward)),
        "rows_in": deep_table(rows_in),
        "inverse": np.stack(split_table(inverse)),
        "rows_out": deep_table(rows_out),
        "up_cols": np.stack(split_table(up_cols)),
        "up_rows": deep_table(up_rows),
        "down_rows": deep_table(up_rows.T),
        "down_cols": np.stack(split_table(up_cols.T)),
        "rows_back": deep_table(rows_out.T),
        "inverse_back": np.stack(split_table(inverse.T)),
        "rows_own": deep_table(own.T),
        "rows_near": deep_table(rows_near),
        "forward_back": np.stack(split_table(forward.T)),
    }


def split(values):
    high = values.astype(jnp.bfloat16)
    low = (values - high.astype(jnp.float32)).astype(jnp.bfloat16)
    return high, low


def dot(left, right):
    return jnp.dot(left, right, preferred_element_type=jnp.float32)


def times_table(values, table):
    rows = values.shape[0]
    high, low = split(values)
    both = dot(jnp.concatenate([high, low], axis=0), table[0])
    return both[:rows] + (both[rows:] + dot(high, table[1]))


def table_times(deep, values):
    high, low = split(values)
    return dot(deep, jnp.concatenate([high, low, high], axis=0))


def fold(product):
    half_rows, half_cols = product.shape[0] // 2, product.shape[1] // 2
    real = product[:half_rows, :half_cols] + product[half_rows:, half_cols:]
    imag = product[:half_rows, half_cols:] - product[half_rows:, :half_cols]
    return jnp.concatenate([real, imag], axis=1)


def unfold(spectrum):
    half = spectrum.shape[1] // 2
    real, imag = spectrum[:, :half], spectrum[:, half:]
    return jnp.concatenate(
        [spectrum, jnp.concatenate([-imag, real], axis=1)], axis=0
    )


def kernel(count, names, weights_ref, mask_hbm, target_hbm, spectra_hbm, *refs):
    tables_hbm = refs[: len(names)]
    refs = refs[len(names) :]
    resist_hbm, grad_hbm = refs[:2]
    refs = refs[2:]
    tables = dict(zip(names, refs[: len(names)]))
    refs = refs[len(names) :]
    (mask, target, spectra, transmit, fields, resist, grad,
     send1, recv1, send2, recv2, in_sem, out_sem, send_sem, recv_sem) = refs

    me = lax.axis_index("tiles")
    following = lax.rem(me + 1, count)
    previous = lax.rem(me + count - 1, count)
    barrier = pltpu.get_barrier_semaphore()
    for other in (previous, following):
        pl.semaphore_signal(barrier, inc=1, device_id={"tiles": other}, device_id_type=MESH)

    sources = {"mask": (mask_hbm, mask), "spectra": (spectra_hbm, spectra), "target": (target_hbm, target)}
    for name, source in zip(names, tables_hbm):
        sources[name] = (source, tables[name])
    order = ["mask", "forward", "rows_in", "spectra", "inverse", "rows_out", "up_cols",
             "up_rows", "target", "down_rows", "down_cols", "rows_back", "inverse_back",
             "rows_own", "rows_near", "forward_back"]
    loads = {}
    for at, name in enumerate(order):
        loads[name] = pltpu.make_async_copy(*sources[name], in_sem.at[at])
        loads[name].start()

    def table(name):
        loads[name].wait()
        return tables[name]

    def swap(step, to_previous, to_following):
        landed = recv1 if step == 0 else recv2
        copies = [
            pltpu.make_async_remote_copy(
                src_ref=to_following, dst_ref=landed.at[0],
                send_sem=send_sem.at[2 * step], recv_sem=recv_sem.at[2 * step],
                device_id={"tiles": following}, device_id_type=MESH),
            pltpu.make_async_remote_copy(
                src_ref=to_previous, dst_ref=landed.at[1],
                send_sem=send_sem.at[2 * step + 1], recv_sem=recv_sem.at[2 * step + 1],
                device_id={"tiles": previous}, device_id_type=MESH),
        ]
        for copy in copies:
            copy.start()
        return copies

    loads["mask"].wait()
    transmit[...] = jnp.tanh(mask[...])
    column_spec = times_table(transmit[...], table("forward"))
    product = table_times(table("rows_in")[...], column_spec)
    span = product.shape[0] // 3
    send1[0] = fold(product[:span])
    send1[1] = fold(product[span : 2 * span])
    pl.semaphore_wait(barrier, 2)
    copies = swap(0, send1.at[0], send1.at[1])
    own_spec = fold(product[2 * span :])

    kernels, freq_rows, freq_cols = spectra.shape[1:]
    loads["spectra"].wait()
    weights = [jnp.full((1, freq_cols), weights_ref[k], jnp.float32) for k in range(kernels)]
    total = functools.reduce(jnp.add, weights)
    for k in range(kernels):
        scale = jnp.sqrt(weights[k] / total)
        spectra[0, k] = spectra[0, k] * scale
        spectra[1, k] = spectra[1, k] * scale
    inverse, rows_out = table("inverse"), table("rows_out")

    for copy in copies:
        copy.wait()
    spec = own_spec + (recv1[0] + recv1[1])
    spec_real, spec_imag = spec[:, :freq_cols], spec[:, freq_cols:]

    depth = 2 * freq_rows
    coarse = fields.shape[1] // 2
    power = None
    for first in range(0, kernels, GROUP):
        members = range(first, min(first + GROUP, kernels))
        blocks = []
        for k in members:
            real = spectra[0, k] * spec_real - spectra[1, k] * spec_imag
            imag = spectra[0, k] * spec_imag + spectra[1, k] * spec_real
            blocks.append(jnp.concatenate([real, imag], axis=1))
            blocks.append(jnp.concatenate([imag, -real], axis=1))
        across = times_table(jnp.concatenate(blocks, axis=0), inverse)
        for place, k in enumerate(members):
            field = table_times(rows_out[...], across[place * depth : (place + 1) * depth])
            fields[k] = field
            term = field[:coarse] * field[:coarse] + field[coarse:] * field[coarse:]
            power = term if power is None else power + term

    intensity = table_times(table("up_rows")[...], times_table(power, table("up_cols")))
    image = jax.nn.sigmoid(STEEPNESS * (intensity - THRESHOLD))
    resist[...] = image
    store_resist = pltpu.make_async_copy(resist, resist_hbm, out_sem.at[0])
    store_resist.start()
    loads["target"].wait()
    slopes = (4.0 * STEEPNESS) * (image - target[...].astype(jnp.float32)) * image * (1.0 - image)
    slopes = times_table(table_times(table("down_rows")[...], slopes), table("down_cols"))
    slopes = jnp.concatenate([slopes, slopes], axis=0)

    rows_back, inverse_back = table("rows_back"), table("inverse_back")
    grad_real = grad_imag = None
    for first in range(0, kernels, GROUP):
        members = range(first, min(first + GROUP, kernels))
        blocks = [table_times(rows_back[...], fields[k] * slopes) for k in members]
        across = times_table(jnp.concatenate(blocks, axis=0), inverse_back)
        for place, k in enumerate(members):
            upper = across[place * depth : place * depth + freq_rows]
            lower = across[place * depth + freq_rows : (place + 1) * depth]
            real = upper[:, :freq_cols] - lower[:, freq_cols:]
            imag = upper[:, freq_cols:] + lower[:, :freq_cols]
            term_real = real * spectra[0, k] + imag * spectra[1, k]
            term_imag = imag * spectra[0, k] - real * spectra[1, k]
            grad_real = term_real if grad_real is None else grad_real + term_real
            grad_imag = term_imag if grad_imag is None else grad_imag + term_imag
    window_grad = jnp.concatenate([grad_real, grad_imag], axis=1)
    send2[...] = window_grad
    copies = swap(1, send2, send2)
    merged = table_times(table("rows_own")[...], unfold(window_grad))
    rows_near, forward_back = table("rows_near"), table("forward_back")
    for copy in copies:
        copy.wait()
    near = jnp.concatenate([unfold(recv2[0]), unfold(recv2[1])], axis=0)
    merged = merged + table_times(rows_near[...], near)
    held = transmit[...]
    grad[...] = times_table(merged, forward_back) * (1.0 - held * held)
    store_grad = pltpu.make_async_copy(grad, grad_hbm, out_sem.at[1])
    store_grad.start()
    store_resist.wait()
    store_grad.wait()


def shards(count, mask_params, target, kernel_spectra, kernel_weights):
    strip_rows, columns = mask_params.shape
    kernels, freq_rows, freq_cols = kernel_spectra.shape[1:]
    tables = make_tables(strip_rows, columns, freq_rows, freq_cols)
    names = list(tables)
    spectrum = (freq_rows, 2 * freq_cols)
    anywhere = pl.BlockSpec(memory_space=pl.ANY)
    out = jax.ShapeDtypeStruct((strip_rows, columns), jnp.float32)
    return pl.pallas_call(
        functools.partial(kernel, count, names),
        out_shape=(out, out),
        in_specs=[pl.BlockSpec(memory_space=pltpu.SMEM)] + [anywhere] * (3 + len(names)),
        out_specs=(anywhere, anywhere),
        scratch_shapes=[pltpu.VMEM(t.shape, jnp.bfloat16) for t in tables.values()]
        + [
            pltpu.VMEM((strip_rows, columns), jnp.float32),
            pltpu.VMEM((strip_rows, columns), jnp.int32),
            pltpu.VMEM(kernel_spectra.shape, jnp.float32),
            pltpu.VMEM((strip_rows, columns), jnp.float32),
            pltpu.VMEM((kernels, 4 * freq_rows, 2 * freq_cols), jnp.float32),
            pltpu.VMEM((strip_rows, columns), jnp.float32),
            pltpu.VMEM((strip_rows, columns), jnp.float32),
            pltpu.VMEM((2,) + spectrum, jnp.float32),
            pltpu.VMEM((2,) + spectrum, jnp.float32),
            pltpu.VMEM(spectrum, jnp.float32),
            pltpu.VMEM((2,) + spectrum, jnp.float32),
            pltpu.SemaphoreType.DMA((3 + len(names),)),
            pltpu.SemaphoreType.DMA((2,)),
            pltpu.SemaphoreType.DMA((4,)),
            pltpu.SemaphoreType.DMA((4,)),
        ],
        compiler_params=pltpu.CompilerParams(
            collective_id=0, has_side_effects=True, vmem_limit_bytes=56 * 1024 * 1024
        ),
        name="litho_step",
    )(kernel_weights, mask_params, target, kernel_spectra, *[jnp.asarray(t) for t in tables.values()])


def solution(mesh):
    rows = P(("parts", "tiles"), None)
    body = functools.partial(shards, mesh.shape["tiles"])
    return jax.shard_map(
        body, mesh=mesh, in_specs=(rows, rows, P(), P()), out_specs=(rows, rows), check_vma=False
    )
```

```python
import functools
import math

import jax
import jax.numpy as jnp
import ml_dtypes
import numpy as np
from jax import lax
from jax.experimental import pallas as pl
from jax.experimental.pallas import tpu as pltpu
from jax.sharding import PartitionSpec as P

MARGIN = 64
STEEPNESS = 8.0
THRESHOLD = 0.35
GROUP = 4
MESH = pl.DeviceIdType.MESH


def split_table(table):
    high = table.astype(ml_dtypes.bfloat16)
    low = (table - high.astype(np.float64)).astype(ml_dtypes.bfloat16)
    return high, low


def deep_table(table):
    high, low = split_table(table)
    return np.concatenate([high, high, low], axis=1)


def cos_sin(frequencies, positions):
    angles = 2.0 * math.pi * np.outer(frequencies, positions)
    return np.cos(angles), np.sin(angles)


def interpolation(half_band, coarse, fine_positions):
    degrees = np.arange(1, half_band)
    offsets = fine_positions[:, None] - (np.arange(coarse) / coarse)[None, :]
    waves = np.cos(2.0 * math.pi * offsets[:, :, None] * degrees).sum(axis=2)
    return (1.0 + 2.0 * waves) / coarse


def make_tables(strip_rows, columns, freq_rows, freq_cols):
    margin = MARGIN
    window = strip_rows + 2 * margin
    col_freq = np.arange(freq_cols) - freq_cols // 2
    row_freq = np.arange(freq_rows) - freq_rows // 2
    col_cos, col_sin = cos_sin(col_freq, np.arange(columns) / columns)
    row_cos, row_sin = cos_sin(row_freq, np.arange(window) / window)
    factor = 1.0 / math.sqrt(window * columns)
    forward = np.concatenate([col_cos.T, -col_sin.T], axis=1) * factor
    stack = np.concatenate([row_cos, row_sin], axis=0)
    own = stack[:, margin : margin + strip_rows]
    to_prev = np.zeros_like(own)
    to_prev[:, :margin] = stack[:, margin + strip_rows :]
    to_next = np.zeros_like(own)
    to_next[:, strip_rows - margin :] = stack[:, :margin]
    rows_in = np.concatenate([to_prev, to_next, own], axis=0)
    rows_near = np.concatenate([to_prev, to_next], axis=0).T
    coarse_rows, coarse_cols = 2 * freq_rows, 2 * freq_cols
    ccos, csin = cos_sin(col_freq, np.arange(coarse_cols) / coarse_cols)
    rcos, rsin = cos_sin(row_freq, np.arange(coarse_rows) / coarse_rows)
    inverse = np.concatenate(
        [np.concatenate([ccos, csin], axis=1), np.concatenate([-csin, ccos], axis=1)], axis=0
    )
    rows_out = np.concatenate(
        [np.concatenate([rcos.T, -rsin.T], axis=1), np.concatenate([rsin.T, rcos.T], axis=1)],
        axis=0,
    )
    own_positions = (margin + np.arange(strip_rows)) / window
    up_rows = interpolation(freq_rows, coarse_rows, own_positions)
    up_cols = interpolation(freq_cols, coarse_cols, np.arange(columns) / columns).T
    return {
        "forward": np.stack(split_table(forward)),
        "rows_in": deep_table(rows_in),
        "inverse": np.stack(split_table(inverse)),
        "rows_out": deep_table(rows_out),
        "up_cols": np.stack(split_table(up_cols)),
        "up_rows": deep_table(up_rows),
        "down_rows": deep_table(up_rows.T),
        "down_cols": np.stack(split_table(up_cols.T)),
        "rows_back": deep_table(rows_out.T),
        "inverse_back": np.stack(split_table(inverse.T)),
        "rows_own": deep_table(own.T),
        "rows_near": deep_table(rows_near),
        "forward_back": np.stack(split_table(forward.T)),
    }


def split(values):
    high = values.astype(jnp.bfloat16)
    low = (values - high.astype(jnp.float32)).astype(jnp.bfloat16)
    return high, low


def dot(left, right):
    return jnp.dot(left, right, preferred_element_type=jnp.float32)


def times_table(values, table):
    rows = values.shape[0]
    high, low = split(values)
    both = dot(jnp.concatenate([high, low], axis=0), table[0])
    return both[:rows] + (both[rows:] + dot(high, table[1]))


def table_times(deep, values):
    high, low = split(values)
    return dot(deep, jnp.concatenate([high, low, high], axis=0))


def fold(product):
    half_rows, half_cols = product.shape[0] // 2, product.shape[1] // 2
    real = product[:half_rows, :half_cols] + product[half_rows:, half_cols:]
    imag = product[:half_rows, half_cols:] - product[half_rows:, :half_cols]
    return jnp.concatenate([real, imag], axis=1)


def unfold(spectrum):
    half = spectrum.shape[1] // 2
    real, imag = spectrum[:, :half], spectrum[:, half:]
    return jnp.concatenate(
        [spectrum, jnp.concatenate([-imag, real], axis=1)], axis=0
    )


def kernel(count, names, weights_ref, mask_hbm, target_hbm, spectra_hbm, *refs):
    tables_hbm = refs[: len(names)]
    refs = refs[len(names) :]
    resist_hbm, grad_hbm = refs[:2]
    refs = refs[2:]
    tables = dict(zip(names, refs[: len(names)]))
    refs = refs[len(names) :]
    (mask, target, spectra, transmit, fields, resist, grad,
     send1, recv1, send2, recv2, in_sem, out_sem, send_sem, recv_sem) = refs

    me = lax.axis_index("tiles")
    following = lax.rem(me + 1, count)
    previous = lax.rem(me + count - 1, count)
    barrier = pltpu.get_barrier_semaphore()
    for other in (previous, following):
        pl.semaphore_signal(barrier, inc=1, device_id={"tiles": other}, device_id_type=MESH)

    sources = {"mask": (mask_hbm, mask), "spectra": (spectra_hbm, spectra), "target": (target_hbm, target)}
    for name, source in zip(names, tables_hbm):
        sources[name] = (source, tables[name])
    order = ["mask", "forward", "rows_in", "spectra", "inverse", "rows_out", "up_cols",
             "up_rows", "target", "down_rows", "down_cols", "rows_back", "inverse_back",
             "rows_own", "rows_near", "forward_back"]
    loads = {}
    for at, name in enumerate(order):
        loads[name] = pltpu.make_async_copy(*sources[name], in_sem.at[at])
    for name in order[:4]:
        loads[name].start()

    def table(name):
        loads[name].wait()
        return tables[name]

    def swap(step, to_previous, to_following):
        landed = recv1 if step == 0 else recv2
        copies = [
            pltpu.make_async_remote_copy(
                src_ref=to_following, dst_ref=landed.at[0],
                send_sem=send_sem.at[2 * step], recv_sem=recv_sem.at[2 * step],
                device_id={"tiles": following}, device_id_type=MESH),
            pltpu.make_async_remote_copy(
                src_ref=to_previous, dst_ref=landed.at[1],
                send_sem=send_sem.at[2 * step + 1], recv_sem=recv_sem.at[2 * step + 1],
                device_id={"tiles": previous}, device_id_type=MESH),
        ]
        for copy in copies:
            copy.start()
        return copies

    loads["mask"].wait()
    transmit[...] = jnp.tanh(mask[...])
    forward = table("forward")
    for name in order[4:]:
        loads[name].start()
    column_spec = times_table(transmit[...], forward)
    product = table_times(table("rows_in")[...], column_spec)
    span = product.shape[0] // 3
    send1[0] = fold(product[:span])
    send1[1] = fold(product[span : 2 * span])
    pl.semaphore_wait(barrier, 2)
    copies = swap(0, send1.at[0], send1.at[1])
    own_spec = fold(product[2 * span :])

    kernels, freq_rows, freq_cols = spectra.shape[1:]
    loads["spectra"].wait()
    weights = [jnp.full((1, freq_cols), weights_ref[k], jnp.float32) for k in range(kernels)]
    total = functools.reduce(jnp.add, weights)
    for k in range(kernels):
        scale = jnp.sqrt(weights[k] / total)
        spectra[0, k] = spectra[0, k] * scale
        spectra[1, k] = spectra[1, k] * scale
    inverse, rows_out = table("inverse"), table("rows_out")

    for copy in copies:
        copy.wait()
    spec = own_spec + (recv1[0] + recv1[1])
    spec_real, spec_imag = spec[:, :freq_cols], spec[:, freq_cols:]

    coarse = fields.shape[1] // 2
    power = None
    for first in range(0, kernels, GROUP):
        members = range(first, min(first + GROUP, kernels))
        blocks = []
        for k in members:
            real = spectra[0, k] * spec_real - spectra[1, k] * spec_imag
            imag = spectra[0, k] * spec_imag + spectra[1, k] * spec_real
            blocks.append(jnp.concatenate([real, imag], axis=1))
        across = times_table(jnp.concatenate(blocks, axis=0), inverse)
        half = across.shape[1] // 2
        for place, k in enumerate(members):
            part = across[place * freq_rows : (place + 1) * freq_rows]
            part = jnp.concatenate([part[:, :half], part[:, half:]], axis=0)
            field = table_times(rows_out[...], part)
            fields[k] = field
            term = field[:coarse] * field[:coarse] + field[coarse:] * field[coarse:]
            power = term if power is None else power + term

    intensity = table_times(table("up_rows")[...], times_table(power, table("up_cols")))
    image = jax.nn.sigmoid(STEEPNESS * (intensity - THRESHOLD))
    resist[...] = image
    store_resist = pltpu.make_async_copy(resist, resist_hbm, out_sem.at[0])
    store_resist.start()
    loads["target"].wait()
    slopes = (4.0 * STEEPNESS) * (image - target[...].astype(jnp.float32)) * image * (1.0 - image)
    slopes = times_table(table_times(table("down_rows")[...], slopes), table("down_cols"))
    slopes = jnp.concatenate([slopes, slopes], axis=0)

    rows_back, inverse_back = table("rows_back"), table("inverse_back")
    grad_real = grad_imag = None
    for first in range(0, kernels, GROUP):
        members = range(first, min(first + GROUP, kernels))
        blocks = []
        for k in members:
            part = table_times(rows_back[...], fields[k] * slopes)
            blocks.append(jnp.concatenate([part[:freq_rows], part[freq_rows:]], axis=1))
        across = times_table(jnp.concatenate(blocks, axis=0), inverse_back)
        for place, k in enumerate(members):
            part = across[place * freq_rows : (place + 1) * freq_rows]
            real, imag = part[:, :freq_cols], part[:, freq_cols:]
            term_real = real * spectra[0, k] + imag * spectra[1, k]
            term_imag = imag * spectra[0, k] - real * spectra[1, k]
            grad_real = term_real if grad_real is None else grad_real + term_real
            grad_imag = term_imag if grad_imag is None else grad_imag + term_imag
    window_grad = jnp.concatenate([grad_real, grad_imag], axis=1)
    send2[...] = window_grad
    copies = swap(1, send2, send2)
    merged = table_times(table("rows_own")[...], unfold(window_grad))
    rows_near, forward_back = table("rows_near"), table("forward_back")
    for copy in copies:
        copy.wait()
    near = jnp.concatenate([unfold(recv2[0]), unfold(recv2[1])], axis=0)
    merged = merged + table_times(rows_near[...], near)
    held = transmit[...]
    grad[...] = times_table(merged, forward_back) * (1.0 - held * held)
    store_grad = pltpu.make_async_copy(grad, grad_hbm, out_sem.at[1])
    store_grad.start()
    store_resist.wait()
    store_grad.wait()


def shards(count, mask_params, target, kernel_spectra, kernel_weights):
    strip_rows, columns = mask_params.shape
    kernels, freq_rows, freq_cols = kernel_spectra.shape[1:]
    tables = make_tables(strip_rows, columns, freq_rows, freq_cols)
    names = list(tables)
    spectrum = (freq_rows, 2 * freq_cols)
    anywhere = pl.BlockSpec(memory_space=pl.ANY)
    out = jax.ShapeDtypeStruct((strip_rows, columns), jnp.float32)
    return pl.pallas_call(
        functools.partial(kernel, count, names),
        out_shape=(out, out),
        in_specs=[pl.BlockSpec(memory_space=pltpu.SMEM)] + [anywhere] * (3 + len(names)),
        out_specs=(anywhere, anywhere),
        scratch_shapes=[pltpu.VMEM(t.shape, jnp.bfloat16) for t in tables.values()]
        + [
            pltpu.VMEM((strip_rows, columns), jnp.float32),
            pltpu.VMEM((strip_rows, columns), jnp.int32),
            pltpu.VMEM(kernel_spectra.shape, jnp.float32),
            pltpu.VMEM((strip_rows, columns), jnp.float32),
            pltpu.VMEM((kernels, 4 * freq_rows, 2 * freq_cols), jnp.float32),
            pltpu.VMEM((strip_rows, columns), jnp.float32),
            pltpu.VMEM((strip_rows, columns), jnp.float32),
            pltpu.VMEM((2,) + spectrum, jnp.float32),
            pltpu.VMEM((2,) + spectrum, jnp.float32),
            pltpu.VMEM(spectrum, jnp.float32),
            pltpu.VMEM((2,) + spectrum, jnp.float32),
            pltpu.SemaphoreType.DMA((3 + len(names),)),
            pltpu.SemaphoreType.DMA((2,)),
            pltpu.SemaphoreType.DMA((4,)),
            pltpu.SemaphoreType.DMA((4,)),
        ],
        compiler_params=pltpu.CompilerParams(
            collective_id=0, has_side_effects=True, vmem_limit_bytes=56 * 1024 * 1024
        ),
        name="litho_step",
    )(kernel_weights, mask_params, target, kernel_spectra, *[jnp.asarray(t) for t in tables.values()])


def solution(mesh):
    rows = P(("parts", "tiles"), None)
    body = functools.partial(shards, mesh.shape["tiles"])
    return jax.shard_map(
        body, mesh=mesh, in_specs=(rows, rows, P(), P()), out_specs=(rows, rows), check_vma=False
    )
```

```python
import functools
import math

import jax
import jax.numpy as jnp
import ml_dtypes
import numpy as np
from jax import lax
from jax.experimental import pallas as pl
from jax.experimental.pallas import tpu as pltpu
from jax.sharding import PartitionSpec as P

MARGIN = 64
STEEPNESS = 8.0
THRESHOLD = 0.35
GROUP = 4
MESH = pl.DeviceIdType.MESH


def split_table(table):
    high = table.astype(ml_dtypes.bfloat16)
    low = (table - high.astype(np.float64)).astype(ml_dtypes.bfloat16)
    return high, low


def deep_table(table):
    high, low = split_table(table)
    return np.concatenate([high, high, low], axis=1)


def cos_sin(frequencies, positions):
    angles = 2.0 * math.pi * np.outer(frequencies, positions)
    return np.cos(angles), np.sin(angles)


def interpolation(half_band, coarse, fine_positions):
    degrees = np.arange(1, half_band)
    offsets = fine_positions[:, None] - (np.arange(coarse) / coarse)[None, :]
    waves = np.cos(2.0 * math.pi * offsets[:, :, None] * degrees).sum(axis=2)
    return (1.0 + 2.0 * waves) / coarse


def make_tables(strip_rows, columns, freq_rows, freq_cols):
    margin = MARGIN
    window = strip_rows + 2 * margin
    col_freq = np.arange(freq_cols) - freq_cols // 2
    row_freq = np.arange(freq_rows) - freq_rows // 2
    col_cos, col_sin = cos_sin(col_freq, np.arange(columns) / columns)
    row_cos, row_sin = cos_sin(row_freq, np.arange(window) / window)
    factor = 1.0 / math.sqrt(window * columns)
    forward = np.concatenate([col_cos.T, -col_sin.T], axis=1) * factor
    stack = np.concatenate([row_cos, row_sin], axis=0)
    own = stack[:, margin : margin + strip_rows]
    to_prev = np.zeros_like(own)
    to_prev[:, :margin] = stack[:, margin + strip_rows :]
    to_next = np.zeros_like(own)
    to_next[:, strip_rows - margin :] = stack[:, :margin]
    rows_in = np.concatenate([to_prev, to_next, own], axis=0)
    rows_near = np.concatenate([to_prev, to_next], axis=0).T
    coarse_rows, coarse_cols = 2 * freq_rows, 2 * freq_cols
    ccos, csin = cos_sin(col_freq, np.arange(coarse_cols) / coarse_cols)
    rcos, rsin = cos_sin(row_freq, np.arange(coarse_rows) / coarse_rows)
    inverse = np.concatenate(
        [np.concatenate([ccos, csin], axis=1), np.concatenate([-csin, ccos], axis=1)], axis=0
    )
    rows_out = np.concatenate(
        [np.concatenate([rcos.T, -rsin.T], axis=1), np.concatenate([rsin.T, rcos.T], axis=1)],
        axis=0,
    )
    own_positions = (margin + np.arange(strip_rows)) / window
    up_rows = interpolation(freq_rows, coarse_rows, own_positions)
    up_cols = interpolation(freq_cols, coarse_cols, np.arange(columns) / columns).T
    return {
        "forward": np.stack(split_table(forward)),
        "rows_in": deep_table(rows_in),
        "inverse": np.stack(split_table(inverse)),
        "rows_out": deep_table(rows_out),
        "up_cols": np.stack(split_table(up_cols)),
        "up_rows": deep_table(up_rows),
        "down_rows": deep_table(up_rows.T),
        "down_cols": np.stack(split_table(up_cols.T)),
        "rows_back": deep_table(rows_out.T),
        "inverse_back": np.stack(split_table(inverse.T)),
        "rows_own": deep_table(own.T),
        "rows_near": deep_table(rows_near),
        "forward_back": np.stack(split_table(forward.T)),
    }


def split(values):
    high = values.astype(jnp.bfloat16)
    low = (values - high.astype(jnp.float32)).astype(jnp.bfloat16)
    return high, low


def dot(left, right):
    return jnp.dot(left, right, preferred_element_type=jnp.float32)


def times_table(values, table):
    rows = values.shape[0]
    high, low = split(values)
    both = dot(jnp.concatenate([high, low], axis=0), table[0])
    return both[:rows] + (both[rows:] + dot(high, table[1]))


def table_times(deep, values):
    high, low = split(values)
    return dot(deep, jnp.concatenate([high, low, high], axis=0))


def fold(product):
    half_rows, half_cols = product.shape[0] // 2, product.shape[1] // 2
    real = product[:half_rows, :half_cols] + product[half_rows:, half_cols:]
    imag = product[:half_rows, half_cols:] - product[half_rows:, :half_cols]
    return jnp.concatenate([real, imag], axis=1)


def unfold(spectrum):
    half = spectrum.shape[1] // 2
    real, imag = spectrum[:, :half], spectrum[:, half:]
    return jnp.concatenate(
        [spectrum, jnp.concatenate([-imag, real], axis=1)], axis=0
    )


def kernel(count, names, weights_ref, mask_hbm, target_hbm, spectra_hbm, *refs):
    tables_hbm = refs[: len(names)]
    refs = refs[len(names) :]
    resist, grad = refs[:2]
    refs = refs[2:]
    tables = dict(zip(names, refs[: len(names)]))
    refs = refs[len(names) :]
    (mask, target, spectra, transmit, fields,
     send1, recv1, send2, recv2, in_sem, send_sem, recv_sem) = refs

    me = lax.axis_index("tiles")
    following = lax.rem(me + 1, count)
    previous = lax.rem(me + count - 1, count)
    barrier = pltpu.get_barrier_semaphore()
    for other in (previous, following):
        pl.semaphore_signal(barrier, inc=1, device_id={"tiles": other}, device_id_type=MESH)

    sources = {"mask": (mask_hbm, mask), "spectra": (spectra_hbm, spectra), "target": (target_hbm, target)}
    for name, source in zip(names, tables_hbm):
        sources[name] = (source, tables[name])
    order = ["mask", "forward", "rows_in", "spectra", "inverse", "rows_out", "up_cols",
             "up_rows", "target", "down_rows", "down_cols", "rows_back", "inverse_back",
             "rows_own", "rows_near", "forward_back"]
    loads = {}
    for at, name in enumerate(order):
        loads[name] = pltpu.make_async_copy(*sources[name], in_sem.at[at])
    for name in order[:4]:
        loads[name].start()

    def table(name):
        loads[name].wait()
        return tables[name]

    def swap(step, to_previous, to_following):
        landed = recv1 if step == 0 else recv2
        copies = [
            pltpu.make_async_remote_copy(
                src_ref=to_following, dst_ref=landed.at[0],
                send_sem=send_sem.at[2 * step], recv_sem=recv_sem.at[2 * step],
                device_id={"tiles": following}, device_id_type=MESH),
            pltpu.make_async_remote_copy(
                src_ref=to_previous, dst_ref=landed.at[1],
                send_sem=send_sem.at[2 * step + 1], recv_sem=recv_sem.at[2 * step + 1],
                device_id={"tiles": previous}, device_id_type=MESH),
        ]
        for copy in copies:
            copy.start()
        return copies

    loads["mask"].wait()
    transmit[...] = jnp.tanh(mask[...])
    forward = table("forward")
    for name in order[4:]:
        loads[name].start()
    column_spec = times_table(transmit[...], forward)
    product = table_times(table("rows_in")[...], column_spec)
    span = product.shape[0] // 3
    send1[0] = fold(product[:span])
    send1[1] = fold(product[span : 2 * span])
    pl.semaphore_wait(barrier, 2)
    copies = swap(0, send1.at[0], send1.at[1])
    own_spec = fold(product[2 * span :])

    kernels, freq_rows, freq_cols = spectra.shape[1:]
    loads["spectra"].wait()
    weights = [jnp.full((1, freq_cols), weights_ref[k], jnp.float32) for k in range(kernels)]
    total = functools.reduce(jnp.add, weights)
    for k in range(kernels):
        scale = jnp.sqrt(weights[k] / total)
        spectra[0, k] = spectra[0, k] * scale
        spectra[1, k] = spectra[1, k] * scale
    inverse, rows_out = table("inverse"), table("rows_out")

    for copy in copies:
        copy.wait()
    spec = own_spec + (recv1[0] + recv1[1])
    spec_real, spec_imag = spec[:, :freq_cols], spec[:, freq_cols:]

    coarse = fields.shape[1] // 2
    power = None
    for first in range(0, kernels, GROUP):
        members = range(first, min(first + GROUP, kernels))
        blocks = []
        for k in members:
            real = spectra[0, k] * spec_real - spectra[1, k] * spec_imag
            imag = spectra[0, k] * spec_imag + spectra[1, k] * spec_real
            blocks.append(jnp.concatenate([real, imag], axis=1))
        across = times_table(jnp.concatenate(blocks, axis=0), inverse)
        half = across.shape[1] // 2
        for place, k in enumerate(members):
            part = across[place * freq_rows : (place + 1) * freq_rows]
            part = jnp.concatenate([part[:, :half], part[:, half:]], axis=0)
            field = table_times(rows_out[...], part)
            fields[k] = field
            term = field[:coarse] * field[:coarse] + field[coarse:] * field[coarse:]
            power = term if power is None else power + term

    intensity = table_times(table("up_rows")[...], times_table(power, table("up_cols")))
    image = jax.nn.sigmoid(STEEPNESS * (intensity - THRESHOLD))
    resist[...] = image
    loads["target"].wait()
    slopes = (4.0 * STEEPNESS) * (image - target[...].astype(jnp.float32)) * image * (1.0 - image)
    slopes = times_table(table_times(table("down_rows")[...], slopes), table("down_cols"))
    slopes = jnp.concatenate([slopes, slopes], axis=0)

    rows_back, inverse_back = table("rows_back"), table("inverse_back")
    grad_real = grad_imag = None
    for first in range(0, kernels, GROUP):
        members = range(first, min(first + GROUP, kernels))
        blocks = []
        for k in members:
            part = table_times(rows_back[...], fields[k] * slopes)
            blocks.append(jnp.concatenate([part[:freq_rows], part[freq_rows:]], axis=1))
        across = times_table(jnp.concatenate(blocks, axis=0), inverse_back)
        for place, k in enumerate(members):
            part = across[place * freq_rows : (place + 1) * freq_rows]
            real, imag = part[:, :freq_cols], part[:, freq_cols:]
            term_real = real * spectra[0, k] + imag * spectra[1, k]
            term_imag = imag * spectra[0, k] - real * spectra[1, k]
            grad_real = term_real if grad_real is None else grad_real + term_real
            grad_imag = term_imag if grad_imag is None else grad_imag + term_imag
    window_grad = jnp.concatenate([grad_real, grad_imag], axis=1)
    send2[...] = window_grad
    copies = swap(1, send2, send2)
    merged = table_times(table("rows_own")[...], unfold(window_grad))
    rows_near, forward_back = table("rows_near"), table("forward_back")
    for copy in copies:
        copy.wait()
    near = jnp.concatenate([unfold(recv2[0]), unfold(recv2[1])], axis=0)
    merged = merged + table_times(rows_near[...], near)
    held = transmit[...]
    grad[...] = times_table(merged, forward_back) * (1.0 - held * held)


def store(resist, grad, resist_hbm, grad_hbm, sems):
    copies = [
        pltpu.make_async_copy(resist, resist_hbm, sems.at[0]),
        pltpu.make_async_copy(grad, grad_hbm, sems.at[1]),
    ]
    for copy in copies:
        copy.start()
    for copy in copies:
        copy.wait()


def shards(count, mask_params, target, kernel_spectra, kernel_weights):
    strip_rows, columns = mask_params.shape
    kernels, freq_rows, freq_cols = kernel_spectra.shape[1:]
    tables = make_tables(strip_rows, columns, freq_rows, freq_cols)
    names = list(tables)
    spectrum = (freq_rows, 2 * freq_cols)
    anywhere = pl.BlockSpec(memory_space=pl.ANY)
    out = jax.ShapeDtypeStruct((strip_rows, columns), jnp.float32)
    held = pltpu.VMEM((strip_rows, columns), jnp.float32)
    in_vmem = pl.BlockSpec(memory_space=pltpu.VMEM)
    resist, grad = pl.pallas_call(
        functools.partial(kernel, count, names),
        out_shape=(held, held),
        in_specs=[pl.BlockSpec(memory_space=pltpu.SMEM)] + [anywhere] * (3 + len(names)),
        out_specs=(in_vmem, in_vmem),
        scratch_shapes=[pltpu.VMEM(t.shape, jnp.bfloat16) for t in tables.values()]
        + [
            pltpu.VMEM((strip_rows, columns), jnp.float32),
            pltpu.VMEM((strip_rows, columns), jnp.int32),
            pltpu.VMEM(kernel_spectra.shape, jnp.float32),
            pltpu.VMEM((strip_rows, columns), jnp.float32),
            pltpu.VMEM((kernels, 4 * freq_rows, 2 * freq_cols), jnp.float32),
            pltpu.VMEM((2,) + spectrum, jnp.float32),
            pltpu.VMEM((2,) + spectrum, jnp.float32),
            pltpu.VMEM(spectrum, jnp.float32),
            pltpu.VMEM((2,) + spectrum, jnp.float32),
            pltpu.SemaphoreType.DMA((3 + len(names),)),
            pltpu.SemaphoreType.DMA((4,)),
            pltpu.SemaphoreType.DMA((4,)),
        ],
        compiler_params=pltpu.CompilerParams(
            collective_id=0, has_side_effects=True, vmem_limit_bytes=56 * 1024 * 1024
        ),
        name="litho_step",
    )(kernel_weights, mask_params, target, kernel_spectra, *[jnp.asarray(t) for t in tables.values()])
    return pl.pallas_call(
        store,
        out_shape=(out, out),
        in_specs=[anywhere, anywhere],
        out_specs=(anywhere, anywhere),
        scratch_shapes=[pltpu.SemaphoreType.DMA((2,))],
        name="store_results",
    )(resist, grad)


def solution(mesh):
    rows = P(("parts", "tiles"), None)
    body = functools.partial(shards, mesh.shape["tiles"])
    return jax.shard_map(
        body, mesh=mesh, in_specs=(rows, rows, P(), P()), out_specs=(rows, rows), check_vma=False
    )
```

```python
import functools
import math

import jax
import jax.numpy as jnp
import ml_dtypes
import numpy as np
from jax import lax
from jax.experimental import pallas as pl
from jax.experimental.pallas import tpu as pltpu
from jax.sharding import PartitionSpec as P

MARGIN = 64
STEEPNESS = 8.0
THRESHOLD = 0.35
GROUP = 4
MESH = pl.DeviceIdType.MESH


def split_table(table):
    high = table.astype(ml_dtypes.bfloat16)
    low = (table - high.astype(np.float64)).astype(ml_dtypes.bfloat16)
    return high, low


def deep_table(table):
    high, low = split_table(table)
    return np.concatenate([high, high, low], axis=1)


def cos_sin(frequencies, positions):
    angles = 2.0 * math.pi * np.outer(frequencies, positions)
    return np.cos(angles), np.sin(angles)


def interpolation(half_band, coarse, fine_positions):
    degrees = np.arange(1, half_band)
    offsets = fine_positions[:, None] - (np.arange(coarse) / coarse)[None, :]
    waves = np.cos(2.0 * math.pi * offsets[:, :, None] * degrees).sum(axis=2)
    return (1.0 + 2.0 * waves) / coarse


def make_tables(strip_rows, columns, freq_rows, freq_cols):
    margin = MARGIN
    window = strip_rows + 2 * margin
    col_freq = np.arange(freq_cols) - freq_cols // 2
    row_freq = np.arange(freq_rows) - freq_rows // 2
    col_cos, col_sin = cos_sin(col_freq, np.arange(columns) / columns)
    row_cos, row_sin = cos_sin(row_freq, np.arange(window) / window)
    factor = 1.0 / math.sqrt(window * columns)
    forward = np.concatenate([col_cos.T, -col_sin.T], axis=1) * factor
    stack = np.concatenate([row_cos, row_sin], axis=0)
    own = stack[:, margin : margin + strip_rows]
    to_prev = np.zeros_like(own)
    to_prev[:, :margin] = stack[:, margin + strip_rows :]
    to_next = np.zeros_like(own)
    to_next[:, strip_rows - margin :] = stack[:, :margin]
    rows_in = np.concatenate([to_prev, to_next, own], axis=0)
    rows_near = np.concatenate([to_prev, to_next], axis=0).T
    coarse_rows, coarse_cols = 2 * freq_rows, 2 * freq_cols
    ccos, csin = cos_sin(col_freq, np.arange(coarse_cols) / coarse_cols)
    rcos, rsin = cos_sin(row_freq, np.arange(coarse_rows) / coarse_rows)
    inverse = np.concatenate(
        [np.concatenate([ccos, csin], axis=1), np.concatenate([-csin, ccos], axis=1)], axis=0
    )
    rows_out = np.concatenate(
        [np.concatenate([rcos.T, -rsin.T], axis=1), np.concatenate([rsin.T, rcos.T], axis=1)],
        axis=0,
    )
    own_positions = (margin + np.arange(strip_rows)) / window
    up_rows = interpolation(freq_rows, coarse_rows, own_positions)
    up_cols = interpolation(freq_cols, coarse_cols, np.arange(columns) / columns).T
    return {
        "forward": np.stack(split_table(forward)),
        "rows_in": deep_table(rows_in),
        "inverse": np.stack(split_table(inverse)),
        "rows_out": deep_table(rows_out),
        "up_cols": np.stack(split_table(up_cols)),
        "up_rows": deep_table(up_rows),
        "down_rows": deep_table(up_rows.T),
        "down_cols": np.stack(split_table(up_cols.T)),
        "rows_back": deep_table(rows_out.T),
        "inverse_back": np.stack(split_table(inverse.T)),
        "rows_own": deep_table(own.T),
        "rows_near": deep_table(rows_near),
        "forward_back": np.stack(split_table(forward.T)),
    }


def split(values):
    high = values.astype(jnp.bfloat16)
    low = (values - high.astype(jnp.float32)).astype(jnp.bfloat16)
    return high, low


def dot(left, right):
    return jnp.dot(left, right, preferred_element_type=jnp.float32)


def times_table(values, table):
    rows = values.shape[0]
    high, low = split(values)
    both = dot(jnp.concatenate([high, low], axis=0), table[0])
    return both[:rows] + (both[rows:] + dot(high, table[1]))


def table_times(deep, values):
    high, low = split(values)
    return dot(deep, jnp.concatenate([high, low, high], axis=0))


def fold(product):
    half_rows, half_cols = product.shape[0] // 2, product.shape[1] // 2
    real = product[:half_rows, :half_cols] + product[half_rows:, half_cols:]
    imag = product[:half_rows, half_cols:] - product[half_rows:, :half_cols]
    return jnp.concatenate([real, imag], axis=1)


def unfold(spectrum):
    half = spectrum.shape[1] // 2
    real, imag = spectrum[:, :half], spectrum[:, half:]
    return jnp.concatenate(
        [spectrum, jnp.concatenate([-imag, real], axis=1)], axis=0
    )


def kernel(count, names, weights_ref, mask_hbm, target_hbm, spectra_hbm, *refs):
    tables_hbm = refs[: len(names)]
    refs = refs[len(names) :]
    resist, grad = refs[:2]
    refs = refs[2:]
    tables = dict(zip(names, refs[: len(names)]))
    refs = refs[len(names) :]
    (mask, target, spectra, transmit, fields,
     send1, recv1, send2, recv2, in_sem, send_sem, recv_sem) = refs

    me = lax.axis_index("tiles")
    following = lax.rem(me + 1, count)
    previous = lax.rem(me + count - 1, count)
    barrier = pltpu.get_barrier_semaphore()
    for other in (previous, following):
        pl.semaphore_signal(barrier, inc=1, device_id={"tiles": other}, device_id_type=MESH)

    sources = {"mask": (mask_hbm, mask), "spectra": (spectra_hbm, spectra), "target": (target_hbm, target)}
    for name, source in zip(names, tables_hbm):
        sources[name] = (source, tables[name])
    order = ["mask", "forward", "rows_in", "spectra", "inverse", "rows_out", "up_cols",
             "up_rows", "target", "down_rows", "down_cols", "rows_back", "inverse_back",
             "rows_own", "rows_near", "forward_back"]
    loads = {}
    for at, name in enumerate(order):
        loads[name] = pltpu.make_async_copy(*sources[name], in_sem.at[at])
    for name in order[:4]:
        loads[name].start()

    def table(name):
        loads[name].wait()
        return tables[name]

    def swap(step, to_previous, to_following):
        landed = recv1 if step == 0 else recv2
        copies = [
            pltpu.make_async_remote_copy(
                src_ref=to_following, dst_ref=landed.at[0],
                send_sem=send_sem.at[2 * step], recv_sem=recv_sem.at[2 * step],
                device_id={"tiles": following}, device_id_type=MESH),
            pltpu.make_async_remote_copy(
                src_ref=to_previous, dst_ref=landed.at[1],
                send_sem=send_sem.at[2 * step + 1], recv_sem=recv_sem.at[2 * step + 1],
                device_id={"tiles": previous}, device_id_type=MESH),
        ]
        for copy in copies:
            copy.start()
        return copies

    loads["mask"].wait()
    transmit[...] = jnp.tanh(mask[...])
    forward = table("forward")
    for name in order[4:]:
        loads[name].start()
    column_spec = times_table(transmit[...], forward)
    product = table_times(table("rows_in")[...], column_spec)
    span = product.shape[0] // 3
    send1[0] = fold(product[:span])
    send1[1] = fold(product[span : 2 * span])
    pl.semaphore_wait(barrier, 2)
    copies = swap(0, send1.at[0], send1.at[1])
    own_spec = fold(product[2 * span :])

    kernels, freq_rows, freq_cols = spectra.shape[1:]
    loads["spectra"].wait()
    weights = [jnp.full((1, freq_cols), weights_ref[k], jnp.float32) for k in range(kernels)]
    total = functools.reduce(jnp.add, weights)
    for k in range(kernels):
        scale = jnp.sqrt(weights[k] / total)
        spectra[0, k] = spectra[0, k] * scale
        spectra[1, k] = spectra[1, k] * scale
    inverse, rows_out = table("inverse"), table("rows_out")

    for copy in copies:
        copy.wait()
    spec = own_spec + (recv1[0] + recv1[1])
    spec_real, spec_imag = spec[:, :freq_cols], spec[:, freq_cols:]

    coarse = fields.shape[1] // 2
    power = None
    for first in range(0, kernels, GROUP):
        members = range(first, min(first + GROUP, kernels))
        blocks = []
        for k in members:
            real = spectra[0, k] * spec_real - spectra[1, k] * spec_imag
            imag = spectra[0, k] * spec_imag + spectra[1, k] * spec_real
            blocks.append(jnp.concatenate([real, imag], axis=1))
        across = times_table(jnp.concatenate(blocks, axis=0), inverse)
        half = across.shape[1] // 2
        for place, k in enumerate(members):
            part = across[place * freq_rows : (place + 1) * freq_rows]
            part = jnp.concatenate([part[:, :half], part[:, half:]], axis=0)
            field = table_times(rows_out[...], part)
            fields[k] = field
            term = field[:coarse] * field[:coarse] + field[coarse:] * field[coarse:]
            power = term if power is None else power + term

    intensity = table_times(table("up_rows")[...], times_table(power, table("up_cols")))
    image = jax.nn.sigmoid(STEEPNESS * (intensity - THRESHOLD))
    resist[...] = image
    loads["target"].wait()
    slopes = (4.0 * STEEPNESS) * (image - target[...].astype(jnp.float32)) * image * (1.0 - image)
    slopes = times_table(table_times(table("down_rows")[...], slopes), table("down_cols"))
    slopes = jnp.concatenate([slopes, slopes], axis=0)

    rows_back, inverse_back = table("rows_back"), table("inverse_back")
    grad_real = grad_imag = None
    for first in range(0, kernels, GROUP):
        members = range(first, min(first + GROUP, kernels))
        blocks = []
        for k in members:
            part = table_times(rows_back[...], fields[k] * slopes)
            blocks.append(jnp.concatenate([part[:freq_rows], part[freq_rows:]], axis=1))
        across = times_table(jnp.concatenate(blocks, axis=0), inverse_back)
        for place, k in enumerate(members):
            part = across[place * freq_rows : (place + 1) * freq_rows]
            real, imag = part[:, :freq_cols], part[:, freq_cols:]
            term_real = real * spectra[0, k] + imag * spectra[1, k]
            term_imag = imag * spectra[0, k] - real * spectra[1, k]
            grad_real = term_real if grad_real is None else grad_real + term_real
            grad_imag = term_imag if grad_imag is None else grad_imag + term_imag
    window_grad = jnp.concatenate([grad_real, grad_imag], axis=1)
    send2[...] = window_grad
    copies = swap(1, send2, send2)
    merged = table_times(table("rows_own")[...], unfold(window_grad))
    rows_near, forward_back = table("rows_near"), table("forward_back")
    for copy in copies:
        copy.wait()
    near = jnp.concatenate([unfold(recv2[0]), unfold(recv2[1])], axis=0)
    merged = merged + table_times(rows_near[...], near)
    held = transmit[...]
    grad[...] = times_table(merged, forward_back) * (1.0 - held * held)


def store(resist, grad, resist_hbm, grad_hbm, sems):
    copies = [
        pltpu.make_async_copy(resist, resist_hbm, sems.at[0]),
        pltpu.make_async_copy(grad, grad_hbm, sems.at[1]),
    ]
    for copy in copies:
        copy.start()
    for copy in copies:
        copy.wait()


def shards(count, mask_params, target, kernel_spectra, kernel_weights):
    strip_rows, columns = mask_params.shape
    kernels, freq_rows, freq_cols = kernel_spectra.shape[1:]
    tables = make_tables(strip_rows, columns, freq_rows, freq_cols)
    names = list(tables)
    spectrum = (freq_rows, 2 * freq_cols)
    anywhere = pl.BlockSpec(memory_space=pl.ANY)
    out = jax.ShapeDtypeStruct((strip_rows, columns), jnp.float32)
    held = pltpu.VMEM((strip_rows, columns), jnp.float32)
    in_vmem = pl.BlockSpec(memory_space=pltpu.VMEM)
    resist, grad = pl.pallas_call(
        functools.partial(kernel, count, names),
        out_shape=(held, held),
        in_specs=[pl.BlockSpec(memory_space=pltpu.SMEM)] + [anywhere] * (3 + len(names)),
        out_specs=(in_vmem, in_vmem),
        scratch_shapes=[pltpu.VMEM(t.shape, jnp.bfloat16) for t in tables.values()]
        + [
            pltpu.VMEM((strip_rows, columns), jnp.float32),
            pltpu.VMEM((strip_rows, columns), jnp.int32),
            pltpu.VMEM(kernel_spectra.shape, jnp.float32),
            pltpu.VMEM((strip_rows, columns), jnp.float32),
            pltpu.VMEM((kernels, 4 * freq_rows, 2 * freq_cols), jnp.float32),
            pltpu.VMEM((2,) + spectrum, jnp.float32),
            pltpu.VMEM((2,) + spectrum, jnp.float32),
            pltpu.VMEM(spectrum, jnp.float32),
            pltpu.VMEM((2,) + spectrum, jnp.float32),
            pltpu.SemaphoreType.DMA((3 + len(names),)),
            pltpu.SemaphoreType.DMA((4,)),
            pltpu.SemaphoreType.DMA((4,)),
        ],
        compiler_params=pltpu.CompilerParams(
            collective_id=0, has_side_effects=True, vmem_limit_bytes=56 * 1024 * 1024
        ),
        name="litho_step",
    )(kernel_weights, mask_params, target, kernel_spectra, *[jnp.asarray(t) for t in tables.values()])
    return pl.pallas_call(
        store,
        out_shape=(out, out),
        in_specs=[in_vmem, in_vmem],
        out_specs=(anywhere, anywhere),
        scratch_shapes=[pltpu.SemaphoreType.DMA((2,))],
        name="store_results",
    )(*[pltpu.with_memory_space_constraint(x, pltpu.VMEM) for x in (resist, grad)])


def solution(mesh):
    rows = P(("parts", "tiles"), None)
    body = functools.partial(shards, mesh.shape["tiles"])
    return jax.shard_map(
        body, mesh=mesh, in_specs=(rows, rows, P(), P()), out_specs=(rows, rows), check_vma=False
    )
```

```python
import functools
import math

import jax
import jax.numpy as jnp
import ml_dtypes
import numpy as np
from jax import lax
from jax.experimental import pallas as pl
from jax.experimental.pallas import tpu as pltpu
from jax.sharding import PartitionSpec as P

MARGIN = 64
STEEPNESS = 8.0
THRESHOLD = 0.35
GROUP = 16
MESH = pl.DeviceIdType.MESH


def split_table(table):
    high = table.astype(ml_dtypes.bfloat16)
    low = (table - high.astype(np.float64)).astype(ml_dtypes.bfloat16)
    return high, low


def deep_table(table):
    high, low = split_table(table)
    return np.concatenate([high, high, low], axis=1)


def tall_table(table):
    high, low = split_table(table)
    return np.concatenate(
        [np.concatenate([high, high], axis=1), np.concatenate([low, low], axis=1)], axis=0
    )


def long_table(table):
    high, low = split_table(table)
    return np.concatenate([high, high, low], axis=0)


def cos_sin(frequencies, positions):
    angles = 2.0 * math.pi * np.outer(frequencies, positions)
    return np.cos(angles), np.sin(angles)


def interpolation(half_band, coarse, fine_positions):
    degrees = np.arange(1, half_band)
    offsets = fine_positions[:, None] - (np.arange(coarse) / coarse)[None, :]
    waves = np.cos(2.0 * math.pi * offsets[:, :, None] * degrees).sum(axis=2)
    return (1.0 + 2.0 * waves) / coarse


def make_tables(strip_rows, columns, freq_rows, freq_cols):
    margin = MARGIN
    window = strip_rows + 2 * margin
    col_freq = np.arange(freq_cols) - freq_cols // 2
    row_freq = np.arange(freq_rows) - freq_rows // 2
    col_cos, col_sin = cos_sin(col_freq, np.arange(columns) / columns)
    row_cos, row_sin = cos_sin(row_freq, np.arange(window) / window)
    factor = 1.0 / math.sqrt(window * columns)
    forward = np.concatenate([col_cos.T, -col_sin.T], axis=1) * factor
    stack = np.concatenate([row_cos, row_sin], axis=0)
    own = stack[:, margin : margin + strip_rows]
    to_prev = np.zeros_like(own)
    to_prev[:, :margin] = stack[:, margin + strip_rows :]
    to_next = np.zeros_like(own)
    to_next[:, strip_rows - margin :] = stack[:, :margin]
    rows_in = np.concatenate([to_prev, to_next, own], axis=0)
    rows_near = np.concatenate([to_prev, to_next], axis=0).T
    coarse_rows, coarse_cols = 2 * freq_rows, 2 * freq_cols
    ccos, csin = cos_sin(col_freq, np.arange(coarse_cols) / coarse_cols)
    rcos, rsin = cos_sin(row_freq, np.arange(coarse_rows) / coarse_rows)
    inverse = np.concatenate(
        [np.concatenate([ccos, csin], axis=1), np.concatenate([-csin, ccos], axis=1)], axis=0
    )
    rows_out = np.concatenate(
        [np.concatenate([rcos.T, -rsin.T], axis=1), np.concatenate([rsin.T, rcos.T], axis=1)],
        axis=0,
    )
    own_positions = (margin + np.arange(strip_rows)) / window
    up_rows = interpolation(freq_rows, coarse_rows, own_positions)
    up_cols = interpolation(freq_cols, coarse_cols, np.arange(columns) / columns).T
    return {
        "forward": np.stack(split_table(forward)),
        "rows_in": deep_table(rows_in),
        "inverse": long_table(inverse),
        "rows_out": deep_table(rows_out),
        "up_cols": np.stack(split_table(up_cols)),
        "up_rows": deep_table(up_rows),
        "down_rows": tall_table(up_rows.T),
        "down_cols": np.stack(split_table(up_cols.T)),
        "rows_back": tall_table(rows_out.T),
        "inverse_back": long_table(inverse.T),
        "rows_own": deep_table(own.T),
        "rows_near": deep_table(rows_near),
        "forward_back": np.stack(split_table(forward.T)),
    }


def split(values):
    high = values.astype(jnp.bfloat16)
    low = (values - high.astype(jnp.float32)).astype(jnp.bfloat16)
    return high, low


def dot(left, right):
    return jnp.dot(left, right, preferred_element_type=jnp.float32)


def times_table(values, table):
    rows = values.shape[0]
    high, low = split(values)
    both = dot(jnp.concatenate([high, low], axis=0), table[0])
    return both[:rows] + (both[rows:] + dot(high, table[1]))


def table_times(deep, values):
    high, low = split(values)
    return dot(deep, jnp.concatenate([high, low, high], axis=0))


def times_long(values, long):
    high, low = split(values)
    return dot(jnp.concatenate([high, low, high], axis=1), long)


def tall_times(tall, values):
    product = dot(tall, jnp.concatenate(split(values), axis=0))
    half = product.shape[0] // 2
    return product[:half] + product[half:]


def fold(product):
    half_rows, half_cols = product.shape[0] // 2, product.shape[1] // 2
    real = product[:half_rows, :half_cols] + product[half_rows:, half_cols:]
    imag = product[:half_rows, half_cols:] - product[half_rows:, :half_cols]
    return jnp.concatenate([real, imag], axis=1)


def unfold(spectrum):
    half = spectrum.shape[1] // 2
    real, imag = spectrum[:, :half], spectrum[:, half:]
    return jnp.concatenate(
        [spectrum, jnp.concatenate([-imag, real], axis=1)], axis=0
    )


def kernel(count, names, weights_ref, mask_hbm, target_hbm, spectra_hbm, *refs):
    tables_hbm = refs[: len(names)]
    refs = refs[len(names) :]
    resist, grad = refs[:2]
    refs = refs[2:]
    tables = dict(zip(names, refs[: len(names)]))
    refs = refs[len(names) :]
    (mask, target, spectra, transmit, fields,
     send1, recv1, send2, recv2, in_sem, send_sem, recv_sem) = refs

    me = lax.axis_index("tiles")
    following = lax.rem(me + 1, count)
    previous = lax.rem(me + count - 1, count)
    barrier = pltpu.get_barrier_semaphore()
    for other in (previous, following):
        pl.semaphore_signal(barrier, inc=1, device_id={"tiles": other}, device_id_type=MESH)

    sources = {"mask": (mask_hbm, mask), "spectra": (spectra_hbm, spectra), "target": (target_hbm, target)}
    for name, source in zip(names, tables_hbm):
        sources[name] = (source, tables[name])
    order = ["mask", "forward", "rows_in", "spectra", "inverse", "rows_out", "up_cols",
             "up_rows", "target", "down_rows", "down_cols", "rows_back", "inverse_back",
             "rows_own", "rows_near", "forward_back"]
    loads = {}
    for at, name in enumerate(order):
        loads[name] = pltpu.make_async_copy(*sources[name], in_sem.at[at])
    for name in order[:4]:
        loads[name].start()

    def table(name):
        loads[name].wait()
        return tables[name]

    def swap(step, to_previous, to_following):
        landed = recv1 if step == 0 else recv2
        copies = [
            pltpu.make_async_remote_copy(
                src_ref=to_following, dst_ref=landed.at[0],
                send_sem=send_sem.at[2 * step], recv_sem=recv_sem.at[2 * step],
                device_id={"tiles": following}, device_id_type=MESH),
            pltpu.make_async_remote_copy(
                src_ref=to_previous, dst_ref=landed.at[1],
                send_sem=send_sem.at[2 * step + 1], recv_sem=recv_sem.at[2 * step + 1],
                device_id={"tiles": previous}, device_id_type=MESH),
        ]
        for copy in copies:
            copy.start()
        return copies

    loads["mask"].wait()
    transmit[...] = jnp.tanh(mask[...])
    forward = table("forward")
    for name in order[4:]:
        loads[name].start()
    column_spec = times_table(transmit[...], forward)
    product = table_times(table("rows_in")[...], column_spec)
    span = product.shape[0] // 3
    send1[0] = fold(product[:span])
    send1[1] = fold(product[span : 2 * span])
    pl.semaphore_wait(barrier, 2)
    copies = swap(0, send1.at[0], send1.at[1])
    own_spec = fold(product[2 * span :])

    kernels, freq_rows, freq_cols = spectra.shape[1:]
    loads["spectra"].wait()
    weights = [jnp.full((1, freq_cols), weights_ref[k], jnp.float32) for k in range(kernels)]
    total = functools.reduce(jnp.add, weights)
    for k in range(kernels):
        scale = jnp.sqrt(weights[k] / total)
        spectra[0, k] = spectra[0, k] * scale
        spectra[1, k] = spectra[1, k] * scale
    inverse, rows_out = table("inverse"), table("rows_out")

    for copy in copies:
        copy.wait()
    spec = own_spec + (recv1[0] + recv1[1])
    spec_real, spec_imag = spec[:, :freq_cols], spec[:, freq_cols:]

    coarse = fields.shape[1] // 2
    power = None
    for first in range(0, kernels, GROUP):
        members = range(first, min(first + GROUP, kernels))
        blocks = []
        for k in members:
            real = spectra[0, k] * spec_real - spectra[1, k] * spec_imag
            imag = spectra[0, k] * spec_imag + spectra[1, k] * spec_real
            blocks.append(jnp.concatenate([real, imag], axis=1))
        across = times_long(jnp.concatenate(blocks, axis=0), inverse[...])
        half = across.shape[1] // 2
        for place, k in enumerate(members):
            part = across[place * freq_rows : (place + 1) * freq_rows]
            part = jnp.concatenate([part[:, :half], part[:, half:]], axis=0)
            field = table_times(rows_out[...], part)
            fields[k] = field
            term = field[:coarse] * field[:coarse] + field[coarse:] * field[coarse:]
            power = term if power is None else power + term

    intensity = table_times(table("up_rows")[...], times_table(power, table("up_cols")))
    image = jax.nn.sigmoid(STEEPNESS * (intensity - THRESHOLD))
    resist[...] = image
    loads["target"].wait()
    slopes = (4.0 * STEEPNESS) * (image - target[...].astype(jnp.float32)) * image * (1.0 - image)
    slopes = times_table(tall_times(table("down_rows")[...], slopes), table("down_cols"))
    slopes = jnp.concatenate([slopes, slopes], axis=0)

    rows_back, inverse_back = table("rows_back"), table("inverse_back")
    grad_real = grad_imag = None
    for first in range(0, kernels, GROUP):
        members = range(first, min(first + GROUP, kernels))
        blocks = []
        for k in members:
            part = tall_times(rows_back[...], fields[k] * slopes)
            blocks.append(jnp.concatenate([part[:freq_rows], part[freq_rows:]], axis=1))
        across = times_long(jnp.concatenate(blocks, axis=0), inverse_back[...])
        for place, k in enumerate(members):
            part = across[place * freq_rows : (place + 1) * freq_rows]
            real, imag = part[:, :freq_cols], part[:, freq_cols:]
            term_real = real * spectra[0, k] + imag * spectra[1, k]
            term_imag = imag * spectra[0, k] - real * spectra[1, k]
            grad_real = term_real if grad_real is None else grad_real + term_real
            grad_imag = term_imag if grad_imag is None else grad_imag + term_imag
    window_grad = jnp.concatenate([grad_real, grad_imag], axis=1)
    send2[...] = window_grad
    copies = swap(1, send2, send2)
    merged = table_times(table("rows_own")[...], unfold(window_grad))
    rows_near, forward_back = table("rows_near"), table("forward_back")
    for copy in copies:
        copy.wait()
    near = jnp.concatenate([unfold(recv2[0]), unfold(recv2[1])], axis=0)
    merged = merged + table_times(rows_near[...], near)
    held = transmit[...]
    grad[...] = times_table(merged, forward_back) * (1.0 - held * held)


def store(resist, grad, resist_hbm, grad_hbm, sems):
    copies = [
        pltpu.make_async_copy(resist, resist_hbm, sems.at[0]),
        pltpu.make_async_copy(grad, grad_hbm, sems.at[1]),
    ]
    for copy in copies:
        copy.start()
    for copy in copies:
        copy.wait()


def shards(count, mask_params, target, kernel_spectra, kernel_weights):
    strip_rows, columns = mask_params.shape
    kernels, freq_rows, freq_cols = kernel_spectra.shape[1:]
    tables = make_tables(strip_rows, columns, freq_rows, freq_cols)
    names = list(tables)
    spectrum = (freq_rows, 2 * freq_cols)
    anywhere = pl.BlockSpec(memory_space=pl.ANY)
    out = jax.ShapeDtypeStruct((strip_rows, columns), jnp.float32)
    held = pltpu.VMEM((strip_rows, columns), jnp.float32)
    in_vmem = pl.BlockSpec(memory_space=pltpu.VMEM)
    resist, grad = pl.pallas_call(
        functools.partial(kernel, count, names),
        out_shape=(held, held),
        in_specs=[pl.BlockSpec(memory_space=pltpu.SMEM)] + [anywhere] * (3 + len(names)),
        out_specs=(in_vmem, in_vmem),
        scratch_shapes=[pltpu.VMEM(t.shape, jnp.bfloat16) for t in tables.values()]
        + [
            pltpu.VMEM((strip_rows, columns), jnp.float32),
            pltpu.VMEM((strip_rows, columns), jnp.int32),
            pltpu.VMEM(kernel_spectra.shape, jnp.float32),
            pltpu.VMEM((strip_rows, columns), jnp.float32),
            pltpu.VMEM((kernels, 4 * freq_rows, 2 * freq_cols), jnp.float32),
            pltpu.VMEM((2,) + spectrum, jnp.float32),
            pltpu.VMEM((2,) + spectrum, jnp.float32),
            pltpu.VMEM(spectrum, jnp.float32),
            pltpu.VMEM((2,) + spectrum, jnp.float32),
            pltpu.SemaphoreType.DMA((3 + len(names),)),
            pltpu.SemaphoreType.DMA((4,)),
            pltpu.SemaphoreType.DMA((4,)),
        ],
        compiler_params=pltpu.CompilerParams(
            collective_id=0, has_side_effects=True, vmem_limit_bytes=56 * 1024 * 1024
        ),
        name="litho_step",
    )(kernel_weights, mask_params, target, kernel_spectra, *[jnp.asarray(t) for t in tables.values()])
    return pl.pallas_call(
        store,
        out_shape=(out, out),
        in_specs=[in_vmem, in_vmem],
        out_specs=(anywhere, anywhere),
        scratch_shapes=[pltpu.SemaphoreType.DMA((2,))],
        name="store_results",
    )(*[pltpu.with_memory_space_constraint(x, pltpu.VMEM) for x in (resist, grad)])


def solution(mesh):
    rows = P(("parts", "tiles"), None)
    body = functools.partial(shards, mesh.shape["tiles"])
    return jax.shard_map(
        body, mesh=mesh, in_specs=(rows, rows, P(), P()), out_specs=(rows, rows), check_vma=False
    )
```

```python
import functools
import math

import jax
import jax.numpy as jnp
import ml_dtypes
import numpy as np
from jax import lax
from jax.experimental import pallas as pl
from jax.experimental.pallas import tpu as pltpu
from jax.sharding import PartitionSpec as P

MARGIN = 64
STEEPNESS = 8.0
THRESHOLD = 0.35
GROUP = 16
CHUNKS = 4
MESH = pl.DeviceIdType.MESH


def split_table(table):
    high = table.astype(ml_dtypes.bfloat16)
    low = (table - high.astype(np.float64)).astype(ml_dtypes.bfloat16)
    return high, low


def deep_table(table):
    high, low = split_table(table)
    return np.concatenate([high, high, low], axis=1)


def tall_table(table):
    high, low = split_table(table)
    return np.concatenate(
        [np.concatenate([high, high], axis=1), np.concatenate([low, low], axis=1)], axis=0
    )


def long_table(table):
    high, low = split_table(table)
    return np.concatenate([high, high, low], axis=0)


def cos_sin(frequencies, positions):
    angles = 2.0 * math.pi * np.outer(frequencies, positions)
    return np.cos(angles), np.sin(angles)


def interpolation(half_band, coarse, fine_positions):
    degrees = np.arange(1, half_band)
    offsets = fine_positions[:, None] - (np.arange(coarse) / coarse)[None, :]
    waves = np.cos(2.0 * math.pi * offsets[:, :, None] * degrees).sum(axis=2)
    return (1.0 + 2.0 * waves) / coarse


def make_tables(strip_rows, columns, freq_rows, freq_cols):
    margin = MARGIN
    window = strip_rows + 2 * margin
    col_freq = np.arange(freq_cols) - freq_cols // 2
    row_freq = np.arange(freq_rows) - freq_rows // 2
    col_cos, col_sin = cos_sin(col_freq, np.arange(columns) / columns)
    row_cos, row_sin = cos_sin(row_freq, np.arange(window) / window)
    factor = 1.0 / math.sqrt(window * columns)
    forward = np.concatenate([col_cos.T, -col_sin.T], axis=1) * factor
    stack = np.concatenate([row_cos, row_sin], axis=0)
    own = stack[:, margin : margin + strip_rows]
    to_prev = np.zeros_like(own)
    to_prev[:, :margin] = stack[:, margin + strip_rows :]
    to_next = np.zeros_like(own)
    to_next[:, strip_rows - margin :] = stack[:, :margin]
    rows_in = np.concatenate([to_prev, to_next, own], axis=0)
    rows_near = np.concatenate([to_prev, to_next], axis=0).T
    coarse_rows, coarse_cols = 2 * freq_rows, 2 * freq_cols
    ccos, csin = cos_sin(col_freq, np.arange(coarse_cols) / coarse_cols)
    rcos, rsin = cos_sin(row_freq, np.arange(coarse_rows) / coarse_rows)
    inverse = np.concatenate(
        [np.concatenate([ccos, csin], axis=1), np.concatenate([-csin, ccos], axis=1)], axis=0
    )
    rows_out = np.concatenate(
        [np.concatenate([rcos.T, -rsin.T], axis=1), np.concatenate([rsin.T, rcos.T], axis=1)],
        axis=0,
    )
    own_positions = (margin + np.arange(strip_rows)) / window
    up_rows = interpolation(freq_rows, coarse_rows, own_positions)
    up_cols = interpolation(freq_cols, coarse_cols, np.arange(columns) / columns).T
    return {
        "forward": np.stack(split_table(forward)),
        "rows_in": deep_table(rows_in),
        "inverse": long_table(inverse),
        "rows_out": deep_table(rows_out),
        "up_cols": np.stack(split_table(up_cols)),
        "up_rows": deep_table(up_rows),
        "down_rows": tall_table(up_rows.T),
        "down_cols": np.stack(split_table(up_cols.T)),
        "rows_back": tall_table(rows_out.T),
        "inverse_back": long_table(inverse.T),
        "rows_own": deep_table(own.T),
        "rows_near": deep_table(rows_near),
        "forward_back": np.stack(split_table(forward.T)),
    }


def split(values):
    high = values.astype(jnp.bfloat16)
    low = (values - high.astype(jnp.float32)).astype(jnp.bfloat16)
    return high, low


def dot(left, right):
    return jnp.dot(left, right, preferred_element_type=jnp.float32)


def times_table(values, table, part=slice(None)):
    rows = values.shape[0]
    high, low = split(values)
    both = dot(jnp.concatenate([high, low], axis=0), table[0, part])
    return both[:rows] + (both[rows:] + dot(high, table[1, part]))


def table_times(deep, values):
    high, low = split(values)
    return dot(deep, jnp.concatenate([high, low, high], axis=0))


def times_long(values, long):
    high, low = split(values)
    return dot(jnp.concatenate([high, low, high], axis=1), long)


def tall_times(tall, values):
    product = dot(tall, jnp.concatenate(split(values), axis=0))
    half = product.shape[0] // 2
    return product[:half] + product[half:]


def fold(product):
    half_rows, half_cols = product.shape[0] // 2, product.shape[1] // 2
    real = product[:half_rows, :half_cols] + product[half_rows:, half_cols:]
    imag = product[:half_rows, half_cols:] - product[half_rows:, :half_cols]
    return jnp.concatenate([real, imag], axis=1)


def unfold(spectrum):
    half = spectrum.shape[1] // 2
    real, imag = spectrum[:, :half], spectrum[:, half:]
    return jnp.concatenate(
        [spectrum, jnp.concatenate([-imag, real], axis=1)], axis=0
    )


def kernel(count, names, weights_ref, mask_hbm, target_hbm, spectra_hbm, *refs):
    tables_hbm = refs[: len(names)]
    refs = refs[len(names) :]
    resist, grad = refs[:2]
    refs = refs[2:]
    tables = dict(zip(names, refs[: len(names)]))
    refs = refs[len(names) :]
    (mask, target, spectra, transmit, fields,
     send1, recv1, send2, recv2, in_sem, send_sem, recv_sem) = refs

    me = lax.axis_index("tiles")
    following = lax.rem(me + 1, count)
    previous = lax.rem(me + count - 1, count)
    barrier = pltpu.get_barrier_semaphore()
    for other in (previous, following):
        pl.semaphore_signal(barrier, inc=1, device_id={"tiles": other}, device_id_type=MESH)

    sources = {"spectra": (spectra_hbm, spectra), "target": (target_hbm, target)}
    for name, source in zip(names, tables_hbm):
        sources[name] = (source, tables[name])
    columns = mask.shape[1]
    chunks = CHUNKS if columns % (128 * CHUNKS) == 0 else 1
    parts = [pl.ds(at * (columns // chunks), columns // chunks) for at in range(chunks)]
    loads = {}

    def load(name, source, destination):
        loads[name] = pltpu.make_async_copy(source, destination, in_sem.at[len(loads)])
        loads[name].start()

    def table(name):
        loads[name].wait()
        return tables[name]

    for at, part in enumerate(parts):
        load(("mask", at), mask_hbm.at[:, part], mask.at[:, part])
        load(("forward", at), sources["forward"][0].at[:, part], tables["forward"].at[:, part])
    load("rows_in", *sources["rows_in"])

    def swap(step, to_previous, to_following):
        landed = recv1 if step == 0 else recv2
        copies = [
            pltpu.make_async_remote_copy(
                src_ref=to_following, dst_ref=landed.at[0],
                send_sem=send_sem.at[2 * step], recv_sem=recv_sem.at[2 * step],
                device_id={"tiles": following}, device_id_type=MESH),
            pltpu.make_async_remote_copy(
                src_ref=to_previous, dst_ref=landed.at[1],
                send_sem=send_sem.at[2 * step + 1], recv_sem=recv_sem.at[2 * step + 1],
                device_id={"tiles": previous}, device_id_type=MESH),
        ]
        for copy in copies:
            copy.start()
        return copies

    later = ("spectra", "inverse", "rows_out", "up_cols", "up_rows", "target", "down_rows",
             "down_cols", "rows_back", "inverse_back", "rows_own", "rows_near", "forward_back")

    column_spec = None
    for at, part in enumerate(parts):
        loads["mask", at].wait()
        transmit[:, part] = jnp.tanh(mask[:, part])
        loads["forward", at].wait()
        if at == len(parts) - 1:
            for name in later:
                load(name, *sources[name])
        term = times_table(transmit[:, part], tables["forward"], part)
        column_spec = term if column_spec is None else column_spec + term
    product = table_times(table("rows_in")[...], column_spec)
    span = product.shape[0] // 3
    send1[0] = fold(product[:span])
    send1[1] = fold(product[span : 2 * span])
    pl.semaphore_wait(barrier, 2)
    first_swap = swap(0, send1.at[0], send1.at[1])
    own_spec = fold(product[2 * span :])

    kernels, freq_rows, freq_cols = spectra.shape[1:]
    loads["spectra"].wait()
    weights = [jnp.full((1, freq_cols), weights_ref[k], jnp.float32) for k in range(kernels)]
    total = functools.reduce(jnp.add, weights)
    for k in range(kernels):
        scale = jnp.sqrt(weights[k] / total)
        spectra[0, k] = spectra[0, k] * scale
        spectra[1, k] = spectra[1, k] * scale
    inverse, rows_out = table("inverse"), table("rows_out")

    for copy in first_swap:
        copy.wait_recv()
    spec = own_spec + (recv1[0] + recv1[1])
    spec_real, spec_imag = spec[:, :freq_cols], spec[:, freq_cols:]

    coarse = fields.shape[1] // 2
    power = None
    for first in range(0, kernels, GROUP):
        members = range(first, min(first + GROUP, kernels))
        blocks = []
        for k in members:
            real = spectra[0, k] * spec_real - spectra[1, k] * spec_imag
            imag = spectra[0, k] * spec_imag + spectra[1, k] * spec_real
            blocks.append(jnp.concatenate([real, imag], axis=1))
        across = times_long(jnp.concatenate(blocks, axis=0), inverse[...])
        half = across.shape[1] // 2
        for place, k in enumerate(members):
            part = across[place * freq_rows : (place + 1) * freq_rows]
            part = jnp.concatenate([part[:, :half], part[:, half:]], axis=0)
            field = table_times(rows_out[...], part)
            fields[k] = field
            term = field[:coarse] * field[:coarse] + field[coarse:] * field[coarse:]
            power = term if power is None else power + term

    intensity = table_times(table("up_rows")[...], times_table(power, table("up_cols")))
    image = jax.nn.sigmoid(STEEPNESS * (intensity - THRESHOLD))
    resist[...] = image
    loads["target"].wait()
    slopes = (4.0 * STEEPNESS) * (image - target[...].astype(jnp.float32)) * image * (1.0 - image)
    slopes = times_table(tall_times(table("down_rows")[...], slopes), table("down_cols"))
    slopes = jnp.concatenate([slopes, slopes], axis=0)

    rows_back, inverse_back = table("rows_back"), table("inverse_back")
    grad_real = grad_imag = None
    for first in range(0, kernels, GROUP):
        members = range(first, min(first + GROUP, kernels))
        blocks = []
        for k in members:
            part = tall_times(rows_back[...], fields[k] * slopes)
            blocks.append(jnp.concatenate([part[:freq_rows], part[freq_rows:]], axis=1))
        across = times_long(jnp.concatenate(blocks, axis=0), inverse_back[...])
        for place, k in enumerate(members):
            part = across[place * freq_rows : (place + 1) * freq_rows]
            real, imag = part[:, :freq_cols], part[:, freq_cols:]
            term_real = real * spectra[0, k] + imag * spectra[1, k]
            term_imag = imag * spectra[0, k] - real * spectra[1, k]
            grad_real = term_real if grad_real is None else grad_real + term_real
            grad_imag = term_imag if grad_imag is None else grad_imag + term_imag
    window_grad = jnp.concatenate([grad_real, grad_imag], axis=1)
    send2[...] = window_grad
    second_swap = swap(1, send2, send2)
    merged = table_times(table("rows_own")[...], unfold(window_grad))
    rows_near, forward_back = table("rows_near"), table("forward_back")
    for copy in second_swap:
        copy.wait_recv()
    near = jnp.concatenate([unfold(recv2[0]), unfold(recv2[1])], axis=0)
    merged = merged + table_times(rows_near[...], near)
    held = transmit[...]
    grad[...] = times_table(merged, forward_back) * (1.0 - held * held)
    for copy in first_swap + second_swap:
        copy.wait_send()


def store(resist, grad, resist_hbm, grad_hbm, sems):
    copies = [
        pltpu.make_async_copy(resist, resist_hbm, sems.at[0]),
        pltpu.make_async_copy(grad, grad_hbm, sems.at[1]),
    ]
    for copy in copies:
        copy.start()
    for copy in copies:
        copy.wait()


def shards(count, mask_params, target, kernel_spectra, kernel_weights):
    strip_rows, columns = mask_params.shape
    kernels, freq_rows, freq_cols = kernel_spectra.shape[1:]
    tables = make_tables(strip_rows, columns, freq_rows, freq_cols)
    names = list(tables)
    spectrum = (freq_rows, 2 * freq_cols)
    anywhere = pl.BlockSpec(memory_space=pl.ANY)
    out = jax.ShapeDtypeStruct((strip_rows, columns), jnp.float32)
    held = pltpu.VMEM((strip_rows, columns), jnp.float32)
    in_vmem = pl.BlockSpec(memory_space=pltpu.VMEM)
    resist, grad = pl.pallas_call(
        functools.partial(kernel, count, names),
        out_shape=(held, held),
        in_specs=[pl.BlockSpec(memory_space=pltpu.SMEM)] + [anywhere] * (3 + len(names)),
        out_specs=(in_vmem, in_vmem),
        scratch_shapes=[pltpu.VMEM(t.shape, jnp.bfloat16) for t in tables.values()]
        + [
            pltpu.VMEM((strip_rows, columns), jnp.float32),
            pltpu.VMEM((strip_rows, columns), jnp.int32),
            pltpu.VMEM(kernel_spectra.shape, jnp.float32),
            pltpu.VMEM((strip_rows, columns), jnp.float32),
            pltpu.VMEM((kernels, 4 * freq_rows, 2 * freq_cols), jnp.float32),
            pltpu.VMEM((2,) + spectrum, jnp.float32),
            pltpu.VMEM((2,) + spectrum, jnp.float32),
            pltpu.VMEM(spectrum, jnp.float32),
            pltpu.VMEM((2,) + spectrum, jnp.float32),
            pltpu.SemaphoreType.DMA((2 + 2 * CHUNKS + len(names),)),
            pltpu.SemaphoreType.DMA((4,)),
            pltpu.SemaphoreType.DMA((4,)),
        ],
        compiler_params=pltpu.CompilerParams(
            collective_id=0, has_side_effects=True, vmem_limit_bytes=56 * 1024 * 1024
        ),
        name="litho_step",
    )(kernel_weights, mask_params, target, kernel_spectra, *[jnp.asarray(t) for t in tables.values()])
    return pl.pallas_call(
        store,
        out_shape=(out, out),
        in_specs=[in_vmem, in_vmem],
        out_specs=(anywhere, anywhere),
        scratch_shapes=[pltpu.SemaphoreType.DMA((2,))],
        name="store_results",
    )(*[pltpu.with_memory_space_constraint(x, pltpu.VMEM) for x in (resist, grad)])


def solution(mesh):
    rows = P(("parts", "tiles"), None)
    body = functools.partial(shards, mesh.shape["tiles"])
    return jax.shard_map(
        body, mesh=mesh, in_specs=(rows, rows, P(), P()), out_specs=(rows, rows), check_vma=False
    )
```

```python
import functools
import math

import jax
import jax.numpy as jnp
import ml_dtypes
import numpy as np
from jax import lax
from jax.experimental import pallas as pl
from jax.experimental.pallas import tpu as pltpu
from jax.sharding import PartitionSpec as P

MARGIN = 64
STEEPNESS = 8.0
THRESHOLD = 0.35
GROUP = 4
CHUNKS = 4
MESH = pl.DeviceIdType.MESH


def split_table(table):
    high = table.astype(ml_dtypes.bfloat16)
    low = (table - high.astype(np.float64)).astype(ml_dtypes.bfloat16)
    return high, low


def deep_table(table):
    high, low = split_table(table)
    return np.concatenate([high, high, low], axis=1)


def tall_table(table):
    high, low = split_table(table)
    return np.concatenate(
        [np.concatenate([high, high], axis=1), np.concatenate([low, low], axis=1)], axis=0
    )


def long_table(table):
    high, low = split_table(table)
    return np.concatenate([high, high, low], axis=0)


def cos_sin(frequencies, positions):
    angles = 2.0 * math.pi * np.outer(frequencies, positions)
    return np.cos(angles), np.sin(angles)


def interpolation(half_band, coarse, fine_positions):
    degrees = np.arange(1, half_band)
    offsets = fine_positions[:, None] - (np.arange(coarse) / coarse)[None, :]
    waves = np.cos(2.0 * math.pi * offsets[:, :, None] * degrees).sum(axis=2)
    return (1.0 + 2.0 * waves) / coarse


def make_tables(strip_rows, columns, freq_rows, freq_cols):
    margin = MARGIN
    window = strip_rows + 2 * margin
    col_freq = np.arange(freq_cols) - freq_cols // 2
    row_freq = np.arange(freq_rows) - freq_rows // 2
    col_cos, col_sin = cos_sin(col_freq, np.arange(columns) / columns)
    row_cos, row_sin = cos_sin(row_freq, np.arange(window) / window)
    factor = 1.0 / math.sqrt(window * columns)
    forward = np.concatenate([col_cos.T, -col_sin.T], axis=1) * factor
    stack = np.concatenate([row_cos, row_sin], axis=0)
    own = stack[:, margin : margin + strip_rows]
    to_prev = np.zeros_like(own)
    to_prev[:, :margin] = stack[:, margin + strip_rows :]
    to_next = np.zeros_like(own)
    to_next[:, strip_rows - margin :] = stack[:, :margin]
    rows_in = np.concatenate([to_prev, to_next, own], axis=0)
    rows_near = np.concatenate([to_prev, to_next], axis=0).T
    coarse_rows, coarse_cols = 2 * freq_rows, 2 * freq_cols
    ccos, csin = cos_sin(col_freq, np.arange(coarse_cols) / coarse_cols)
    rcos, rsin = cos_sin(row_freq, np.arange(coarse_rows) / coarse_rows)
    inverse = np.concatenate(
        [np.concatenate([ccos, csin], axis=1), np.concatenate([-csin, ccos], axis=1)], axis=0
    )
    rows_out = np.concatenate(
        [np.concatenate([rcos.T, -rsin.T], axis=1), np.concatenate([rsin.T, rcos.T], axis=1)],
        axis=0,
    )
    own_positions = (margin + np.arange(strip_rows)) / window
    up_rows = interpolation(freq_rows, coarse_rows, own_positions)
    up_cols = interpolation(freq_cols, coarse_cols, np.arange(columns) / columns).T
    return {
        "forward": np.stack(split_table(forward)),
        "rows_in": deep_table(rows_in),
        "inverse": long_table(inverse),
        "rows_out": deep_table(rows_out),
        "up_cols": np.stack(split_table(up_cols)),
        "up_rows": deep_table(up_rows),
        "down_rows": tall_table(up_rows.T),
        "down_cols": np.stack(split_table(up_cols.T)),
        "rows_back": tall_table(rows_out.T),
        "inverse_back": long_table(inverse.T),
        "rows_own": deep_table(own.T),
        "rows_near": deep_table(rows_near),
        "forward_back": np.stack(split_table(forward.T)),
    }


def split(values):
    high = values.astype(jnp.bfloat16)
    low = (values - high.astype(jnp.float32)).astype(jnp.bfloat16)
    return high, low


def dot(left, right):
    return jnp.dot(left, right, preferred_element_type=jnp.float32)


def times_table(values, table, part=slice(None)):
    rows = values.shape[0]
    high, low = split(values)
    both = dot(jnp.concatenate([high, low], axis=0), table[0, part])
    return both[:rows] + (both[rows:] + dot(high, table[1, part]))


def table_times(deep, values):
    high, low = split(values)
    return dot(deep, jnp.concatenate([high, low, high], axis=0))


def times_long(values, long):
    high, low = split(values)
    return dot(jnp.concatenate([high, low, high], axis=1), long)


def tall_times(tall, values):
    product = dot(tall, jnp.concatenate(split(values), axis=0))
    half = product.shape[0] // 2
    return product[:half] + product[half:]


def fold(product):
    half_rows, half_cols = product.shape[0] // 2, product.shape[1] // 2
    real = product[:half_rows, :half_cols] + product[half_rows:, half_cols:]
    imag = product[:half_rows, half_cols:] - product[half_rows:, :half_cols]
    return jnp.concatenate([real, imag], axis=1)


def unfold(spectrum):
    half = spectrum.shape[1] // 2
    real, imag = spectrum[:, :half], spectrum[:, half:]
    return jnp.concatenate(
        [spectrum, jnp.concatenate([-imag, real], axis=1)], axis=0
    )


def kernel(count, names, weights_ref, mask_hbm, target_hbm, spectra_hbm, *refs):
    tables_hbm = refs[: len(names)]
    refs = refs[len(names) :]
    resist, grad = refs[:2]
    refs = refs[2:]
    tables = dict(zip(names, refs[: len(names)]))
    refs = refs[len(names) :]
    (mask, target, spectra, transmit, fields,
     send1, recv1, send2, recv2, in_sem, send_sem, recv_sem) = refs

    me = lax.axis_index("tiles")
    following = lax.rem(me + 1, count)
    previous = lax.rem(me + count - 1, count)
    barrier = pltpu.get_barrier_semaphore()
    for other in (previous, following):
        pl.semaphore_signal(barrier, inc=1, device_id={"tiles": other}, device_id_type=MESH)

    sources = {"spectra": (spectra_hbm, spectra), "target": (target_hbm, target)}
    for name, source in zip(names, tables_hbm):
        sources[name] = (source, tables[name])
    columns = mask.shape[1]
    chunks = CHUNKS if columns % (128 * CHUNKS) == 0 else 1
    parts = [pl.ds(at * (columns // chunks), columns // chunks) for at in range(chunks)]
    loads = {}

    def load(name, source, destination):
        loads[name] = pltpu.make_async_copy(source, destination, in_sem.at[len(loads)])
        loads[name].start()

    def table(name):
        loads[name].wait()
        return tables[name]

    for at, part in enumerate(parts):
        load(("mask", at), mask_hbm.at[:, part], mask.at[:, part])
        load(("forward", at), sources["forward"][0].at[:, part], tables["forward"].at[:, part])
    load("rows_in", *sources["rows_in"])

    def swap(step, to_previous, to_following):
        landed = recv1 if step == 0 else recv2
        copies = [
            pltpu.make_async_remote_copy(
                src_ref=to_following, dst_ref=landed.at[0],
                send_sem=send_sem.at[2 * step], recv_sem=recv_sem.at[2 * step],
                device_id={"tiles": following}, device_id_type=MESH),
            pltpu.make_async_remote_copy(
                src_ref=to_previous, dst_ref=landed.at[1],
                send_sem=send_sem.at[2 * step + 1], recv_sem=recv_sem.at[2 * step + 1],
                device_id={"tiles": previous}, device_id_type=MESH),
        ]
        for copy in copies:
            copy.start()
        return copies

    later = ("spectra", "inverse", "rows_out", "up_cols", "up_rows", "target", "down_rows",
             "down_cols", "rows_back", "inverse_back", "rows_own", "rows_near", "forward_back")

    column_spec = None
    for at, part in enumerate(parts):
        loads["mask", at].wait()
        transmit[:, part] = jnp.tanh(mask[:, part])
        loads["forward", at].wait()
        if at == len(parts) - 1:
            for name in later:
                load(name, *sources[name])
        term = times_table(transmit[:, part], tables["forward"], part)
        column_spec = term if column_spec is None else column_spec + term
    product = table_times(table("rows_in")[...], column_spec)
    span = product.shape[0] // 3
    send1[0] = fold(product[:span])
    send1[1] = fold(product[span : 2 * span])
    pl.semaphore_wait(barrier, 2)
    first_swap = swap(0, send1.at[0], send1.at[1])
    own_spec = fold(product[2 * span :])

    kernels, freq_rows, freq_cols = spectra.shape[1:]
    loads["spectra"].wait()
    weights = [jnp.full((1, freq_cols), weights_ref[k], jnp.float32) for k in range(kernels)]
    total = functools.reduce(jnp.add, weights)
    for k in range(kernels):
        scale = jnp.sqrt(weights[k] / total)
        spectra[0, k] = spectra[0, k] * scale
        spectra[1, k] = spectra[1, k] * scale
    inverse, rows_out = table("inverse"), table("rows_out")

    for copy in first_swap:
        copy.wait_recv()
    spec = own_spec + (recv1[0] + recv1[1])
    spec_real, spec_imag = spec[:, :freq_cols], spec[:, freq_cols:]

    coarse = fields.shape[1] // 2
    width = fields.shape[2] // GROUP
    blocks = []
    for k in range(kernels):
        real = spectra[0, k] * spec_real - spectra[1, k] * spec_imag
        imag = spectra[0, k] * spec_imag + spectra[1, k] * spec_real
        blocks.append(jnp.concatenate([real, imag], axis=1))
    across = times_long(jnp.concatenate(blocks, axis=0), inverse[...])
    power = None
    for group in range(fields.shape[0]):
        blocks = []
        for k in range(group * GROUP, (group + 1) * GROUP):
            part = across[k * freq_rows : (k + 1) * freq_rows]
            blocks.append(jnp.concatenate([part[:, :width], part[:, width:]], axis=0))
        field = table_times(rows_out[...], jnp.concatenate(blocks, axis=1))
        fields[group] = field
        terms = field[:coarse] * field[:coarse] + field[coarse:] * field[coarse:]
        for place in range(GROUP):
            term = terms[:, place * width : (place + 1) * width]
            power = term if power is None else power + term

    intensity = table_times(table("up_rows")[...], times_table(power, table("up_cols")))
    image = jax.nn.sigmoid(STEEPNESS * (intensity - THRESHOLD))
    resist[...] = image
    loads["target"].wait()
    slopes = (4.0 * STEEPNESS) * (image - target[...].astype(jnp.float32)) * image * (1.0 - image)
    slopes = times_table(tall_times(table("down_rows")[...], slopes), table("down_cols"))
    slopes = jnp.concatenate([slopes, slopes], axis=0)
    slopes = jnp.concatenate([slopes] * GROUP, axis=1)

    rows_back, inverse_back = table("rows_back"), table("inverse_back")
    blocks = []
    for group in range(fields.shape[0]):
        part = tall_times(rows_back[...], fields[group] * slopes)
        for place in range(GROUP):
            piece = part[:, place * width : (place + 1) * width]
            blocks.append(jnp.concatenate([piece[:freq_rows], piece[freq_rows:]], axis=1))
    across = times_long(jnp.concatenate(blocks, axis=0), inverse_back[...])
    grad_real = grad_imag = None
    for k in range(kernels):
        part = across[k * freq_rows : (k + 1) * freq_rows]
        real, imag = part[:, :freq_cols], part[:, freq_cols:]
        term_real = real * spectra[0, k] + imag * spectra[1, k]
        term_imag = imag * spectra[0, k] - real * spectra[1, k]
        grad_real = term_real if grad_real is None else grad_real + term_real
        grad_imag = term_imag if grad_imag is None else grad_imag + term_imag
    window_grad = jnp.concatenate([grad_real, grad_imag], axis=1)
    send2[...] = window_grad
    second_swap = swap(1, send2, send2)
    merged = table_times(table("rows_own")[...], unfold(window_grad))
    rows_near, forward_back = table("rows_near"), table("forward_back")
    for copy in second_swap:
        copy.wait_recv()
    near = jnp.concatenate([unfold(recv2[0]), unfold(recv2[1])], axis=0)
    merged = merged + table_times(rows_near[...], near)
    held = transmit[...]
    grad[...] = times_table(merged, forward_back) * (1.0 - held * held)
    for copy in first_swap + second_swap:
        copy.wait_send()


def store(resist, grad, resist_hbm, grad_hbm, sems):
    copies = [
        pltpu.make_async_copy(resist, resist_hbm, sems.at[0]),
        pltpu.make_async_copy(grad, grad_hbm, sems.at[1]),
    ]
    for copy in copies:
        copy.start()
    for copy in copies:
        copy.wait()


def shards(count, mask_params, target, kernel_spectra, kernel_weights):
    strip_rows, columns = mask_params.shape
    kernels, freq_rows, freq_cols = kernel_spectra.shape[1:]
    tables = make_tables(strip_rows, columns, freq_rows, freq_cols)
    names = list(tables)
    spectrum = (freq_rows, 2 * freq_cols)
    anywhere = pl.BlockSpec(memory_space=pl.ANY)
    out = jax.ShapeDtypeStruct((strip_rows, columns), jnp.float32)
    held = pltpu.VMEM((strip_rows, columns), jnp.float32)
    in_vmem = pl.BlockSpec(memory_space=pltpu.VMEM)
    resist, grad = pl.pallas_call(
        functools.partial(kernel, count, names),
        out_shape=(held, held),
        in_specs=[pl.BlockSpec(memory_space=pltpu.SMEM)] + [anywhere] * (3 + len(names)),
        out_specs=(in_vmem, in_vmem),
        scratch_shapes=[pltpu.VMEM(t.shape, jnp.bfloat16) for t in tables.values()]
        + [
            pltpu.VMEM((strip_rows, columns), jnp.float32),
            pltpu.VMEM((strip_rows, columns), jnp.int32),
            pltpu.VMEM(kernel_spectra.shape, jnp.float32),
            pltpu.VMEM((strip_rows, columns), jnp.float32),
            pltpu.VMEM((kernels // GROUP, 4 * freq_rows, GROUP * 2 * freq_cols), jnp.float32),
            pltpu.VMEM((2,) + spectrum, jnp.float32),
            pltpu.VMEM((2,) + spectrum, jnp.float32),
            pltpu.VMEM(spectrum, jnp.float32),
            pltpu.VMEM((2,) + spectrum, jnp.float32),
            pltpu.SemaphoreType.DMA((2 + 2 * CHUNKS + len(names),)),
            pltpu.SemaphoreType.DMA((4,)),
            pltpu.SemaphoreType.DMA((4,)),
        ],
        compiler_params=pltpu.CompilerParams(
            collective_id=0, has_side_effects=True, vmem_limit_bytes=56 * 1024 * 1024
        ),
        name="litho_step",
    )(kernel_weights, mask_params, target, kernel_spectra, *[jnp.asarray(t) for t in tables.values()])
    return pl.pallas_call(
        store,
        out_shape=(out, out),
        in_specs=[in_vmem, in_vmem],
        out_specs=(anywhere, anywhere),
        scratch_shapes=[pltpu.SemaphoreType.DMA((2,))],
        name="store_results",
    )(*[pltpu.with_memory_space_constraint(x, pltpu.VMEM) for x in (resist, grad)])


def solution(mesh):
    rows = P(("parts", "tiles"), None)
    body = functools.partial(shards, mesh.shape["tiles"])
    return jax.shard_map(
        body, mesh=mesh, in_specs=(rows, rows, P(), P()), out_specs=(rows, rows), check_vma=False
    )
```

```python
import functools
import math

import jax
import jax.numpy as jnp
import ml_dtypes
import numpy as np
from jax import lax
from jax.experimental import pallas as pl
from jax.experimental.pallas import tpu as pltpu
from jax.sharding import PartitionSpec as P

MARGIN = 64
STEEPNESS = 8.0
THRESHOLD = 0.35
GROUP = 4
CHUNKS = 4
MESH = pl.DeviceIdType.MESH


def split_table(table):
    high = table.astype(ml_dtypes.bfloat16)
    low = (table - high.astype(np.float64)).astype(ml_dtypes.bfloat16)
    return high, low


def deep_table(table):
    high, low = split_table(table)
    return np.concatenate([high, high, low], axis=1)


def tall_table(table):
    high, low = split_table(table)
    return np.concatenate(
        [np.concatenate([high, high], axis=1), np.concatenate([low, low], axis=1)], axis=0
    )


def cos_sin(frequencies, positions):
    angles = 2.0 * math.pi * np.outer(frequencies, positions)
    return np.cos(angles), np.sin(angles)


def interpolation(half_band, coarse, fine_positions):
    degrees = np.arange(1, half_band)
    offsets = fine_positions[:, None] - (np.arange(coarse) / coarse)[None, :]
    waves = np.cos(2.0 * math.pi * offsets[:, :, None] * degrees).sum(axis=2)
    return (1.0 + 2.0 * waves) / coarse


def make_tables(strip_rows, columns, freq_rows, freq_cols):
    margin = MARGIN
    window = strip_rows + 2 * margin
    col_freq = np.arange(freq_cols) - freq_cols // 2
    row_freq = np.arange(freq_rows) - freq_rows // 2
    col_cos, col_sin = cos_sin(col_freq, np.arange(columns) / columns)
    row_cos, row_sin = cos_sin(row_freq, np.arange(window) / window)
    factor = 1.0 / math.sqrt(window * columns)
    forward = np.concatenate([col_cos.T, -col_sin.T], axis=1) * factor
    stack = np.concatenate([row_cos, row_sin], axis=0)
    own = stack[:, margin : margin + strip_rows]
    to_prev = np.zeros_like(own)
    to_prev[:, :margin] = stack[:, margin + strip_rows :]
    to_next = np.zeros_like(own)
    to_next[:, strip_rows - margin :] = stack[:, :margin]
    rows_in = np.concatenate([to_prev, to_next, own], axis=0)
    rows_near = np.concatenate([to_prev, to_next], axis=0).T
    coarse_rows, coarse_cols = 2 * freq_rows, 2 * freq_cols
    ccos, csin = cos_sin(col_freq, np.arange(coarse_cols) / coarse_cols)
    rcos, rsin = cos_sin(row_freq, np.arange(coarse_rows) / coarse_rows)
    inverse = np.concatenate(
        [np.concatenate([ccos, csin], axis=1), np.concatenate([-csin, ccos], axis=1)], axis=0
    )
    rows_out = np.concatenate(
        [np.concatenate([rcos.T, -rsin.T], axis=1), np.concatenate([rsin.T, rcos.T], axis=1)],
        axis=0,
    )
    own_positions = (margin + np.arange(strip_rows)) / window
    up_rows = interpolation(freq_rows, coarse_rows, own_positions)
    up_cols = interpolation(freq_cols, coarse_cols, np.arange(columns) / columns).T
    return {
        "forward": np.stack(split_table(forward)),
        "rows_in": deep_table(rows_in),
        "inverse": np.stack(split_table(inverse)),
        "rows_out": deep_table(rows_out),
        "up_cols": np.stack(split_table(up_cols)),
        "up_rows": deep_table(up_rows),
        "down_rows": tall_table(up_rows.T),
        "rows_back": tall_table(rows_out.T),
        "rows_own": deep_table(own.T),
        "rows_near": deep_table(rows_near),
    }


def split(values):
    high = values.astype(jnp.bfloat16)
    low = (values - high.astype(jnp.float32)).astype(jnp.bfloat16)
    return high, low


def dot(left, right):
    return jnp.dot(left, right, preferred_element_type=jnp.float32)


def dot_across(left, right):
    return lax.dot_general(
        left, right, (((1,), (1,)), ((), ())), preferred_element_type=jnp.float32
    )


def times_table(values, table, part=slice(None), product=dot):
    rows = values.shape[0]
    high, low = split(values)
    both = product(jnp.concatenate([high, low], axis=0), table[0, part])
    return both[:rows] + (both[rows:] + product(high, table[1, part]))


def table_times(deep, values):
    high, low = split(values)
    return dot(deep, jnp.concatenate([high, low, high], axis=0))


def tall_times(tall, values):
    product = dot(tall, jnp.concatenate(split(values), axis=0))
    half = product.shape[0] // 2
    return product[:half] + product[half:]


def fold(product):
    half_rows, half_cols = product.shape[0] // 2, product.shape[1] // 2
    real = product[:half_rows, :half_cols] + product[half_rows:, half_cols:]
    imag = product[:half_rows, half_cols:] - product[half_rows:, :half_cols]
    return jnp.concatenate([real, imag], axis=1)


def unfold(spectrum):
    half = spectrum.shape[1] // 2
    real, imag = spectrum[:, :half], spectrum[:, half:]
    return jnp.concatenate(
        [spectrum, jnp.concatenate([-imag, real], axis=1)], axis=0
    )


def kernel(count, names, weights_ref, mask_hbm, target_hbm, spectra_hbm, *refs):
    tables_hbm = refs[: len(names)]
    refs = refs[len(names) :]
    resist, grad = refs[:2]
    refs = refs[2:]
    tables = dict(zip(names, refs[: len(names)]))
    refs = refs[len(names) :]
    (mask, target, spectra, transmit, fields,
     send1, recv1, send2, recv2, in_sem, send_sem, recv_sem) = refs

    me = lax.axis_index("tiles")
    following = lax.rem(me + 1, count)
    previous = lax.rem(me + count - 1, count)
    barrier = pltpu.get_barrier_semaphore()
    for other in (previous, following):
        pl.semaphore_signal(barrier, inc=1, device_id={"tiles": other}, device_id_type=MESH)

    sources = {"spectra": (spectra_hbm, spectra), "target": (target_hbm, target)}
    for name, source in zip(names, tables_hbm):
        sources[name] = (source, tables[name])
    columns = mask.shape[1]
    chunks = CHUNKS if columns % (128 * CHUNKS) == 0 else 1
    parts = [pl.ds(at * (columns // chunks), columns // chunks) for at in range(chunks)]
    loads = {}

    def load(name, source, destination):
        loads[name] = pltpu.make_async_copy(source, destination, in_sem.at[len(loads)])
        loads[name].start()

    def table(name):
        loads[name].wait()
        return tables[name]

    for at, part in enumerate(parts):
        load(("mask", at), mask_hbm.at[:, part], mask.at[:, part])
        load(("forward", at), sources["forward"][0].at[:, part], tables["forward"].at[:, part])
    load("rows_in", *sources["rows_in"])

    def swap(step, to_previous, to_following):
        landed = recv1 if step == 0 else recv2
        copies = [
            pltpu.make_async_remote_copy(
                src_ref=to_following, dst_ref=landed.at[0],
                send_sem=send_sem.at[2 * step], recv_sem=recv_sem.at[2 * step],
                device_id={"tiles": following}, device_id_type=MESH),
            pltpu.make_async_remote_copy(
                src_ref=to_previous, dst_ref=landed.at[1],
                send_sem=send_sem.at[2 * step + 1], recv_sem=recv_sem.at[2 * step + 1],
                device_id={"tiles": previous}, device_id_type=MESH),
        ]
        for copy in copies:
            copy.start()
        return copies

    later = ("spectra", "inverse", "rows_out", "up_cols", "up_rows", "target", "down_rows",
             "rows_back", "rows_own", "rows_near")

    column_spec = None
    for at, part in enumerate(parts):
        loads["mask", at].wait()
        transmit[:, part] = jnp.tanh(mask[:, part])
        loads["forward", at].wait()
        if at == len(parts) - 1:
            for name in later:
                load(name, *sources[name])
        term = times_table(transmit[:, part], tables["forward"], part)
        column_spec = term if column_spec is None else column_spec + term
    product = table_times(table("rows_in")[...], column_spec)
    span = product.shape[0] // 3
    send1[0] = fold(product[:span])
    send1[1] = fold(product[span : 2 * span])
    pl.semaphore_wait(barrier, 2)
    first_swap = swap(0, send1.at[0], send1.at[1])
    own_spec = fold(product[2 * span :])

    kernels, freq_rows, freq_cols = spectra.shape[1:]
    loads["spectra"].wait()
    weights = [jnp.full((1, freq_cols), weights_ref[k], jnp.float32) for k in range(kernels)]
    total = functools.reduce(jnp.add, weights)
    for k in range(kernels):
        scale = jnp.sqrt(weights[k] / total)
        spectra[0, k] = spectra[0, k] * scale
        spectra[1, k] = spectra[1, k] * scale
    inverse, rows_out = table("inverse"), table("rows_out")

    for copy in first_swap:
        copy.wait_recv()
    spec = own_spec + (recv1[0] + recv1[1])
    spec_real, spec_imag = spec[:, :freq_cols], spec[:, freq_cols:]

    coarse = fields.shape[1] // 2
    width = fields.shape[2] // GROUP
    blocks = []
    for k in range(kernels):
        real = spectra[0, k] * spec_real - spectra[1, k] * spec_imag
        imag = spectra[0, k] * spec_imag + spectra[1, k] * spec_real
        blocks.append(jnp.concatenate([real, imag], axis=1))
    across = times_table(jnp.concatenate(blocks, axis=0), inverse)
    power = None
    for group in range(fields.shape[0]):
        blocks = []
        for k in range(group * GROUP, (group + 1) * GROUP):
            part = across[k * freq_rows : (k + 1) * freq_rows]
            blocks.append(jnp.concatenate([part[:, :width], part[:, width:]], axis=0))
        field = table_times(rows_out[...], jnp.concatenate(blocks, axis=1))
        fields[group] = field
        terms = field[:coarse] * field[:coarse] + field[coarse:] * field[coarse:]
        for place in range(GROUP):
            term = terms[:, place * width : (place + 1) * width]
            power = term if power is None else power + term

    intensity = table_times(table("up_rows")[...], times_table(power, table("up_cols")))
    image = jax.nn.sigmoid(STEEPNESS * (intensity - THRESHOLD))
    resist[...] = image
    loads["target"].wait()
    slopes = (4.0 * STEEPNESS) * (image - target[...].astype(jnp.float32)) * image * (1.0 - image)
    slopes = tall_times(table("down_rows")[...], slopes)
    slopes = times_table(slopes, tables["up_cols"], product=dot_across)
    slopes = jnp.concatenate([slopes, slopes], axis=0)
    slopes = jnp.concatenate([slopes] * GROUP, axis=1)

    rows_back = table("rows_back")
    blocks = []
    for group in range(fields.shape[0]):
        part = tall_times(rows_back[...], fields[group] * slopes)
        for place in range(GROUP):
            piece = part[:, place * width : (place + 1) * width]
            blocks.append(jnp.concatenate([piece[:freq_rows], piece[freq_rows:]], axis=1))
    across = times_table(jnp.concatenate(blocks, axis=0), inverse, product=dot_across)
    grad_real = grad_imag = None
    for k in range(kernels):
        part = across[k * freq_rows : (k + 1) * freq_rows]
        real, imag = part[:, :freq_cols], part[:, freq_cols:]
        term_real = real * spectra[0, k] + imag * spectra[1, k]
        term_imag = imag * spectra[0, k] - real * spectra[1, k]
        grad_real = term_real if grad_real is None else grad_real + term_real
        grad_imag = term_imag if grad_imag is None else grad_imag + term_imag
    window_grad = jnp.concatenate([grad_real, grad_imag], axis=1)
    send2[...] = window_grad
    second_swap = swap(1, send2, send2)
    merged = table_times(table("rows_own")[...], unfold(window_grad))
    rows_near = table("rows_near")
    for copy in second_swap:
        copy.wait_recv()
    near = jnp.concatenate([unfold(recv2[0]), unfold(recv2[1])], axis=0)
    merged = merged + table_times(rows_near[...], near)
    held = transmit[...]
    grad[...] = times_table(merged, tables["forward"], product=dot_across) * (1.0 - held * held)
    for copy in first_swap + second_swap:
        copy.wait_send()


def store(resist, grad, resist_hbm, grad_hbm, sems):
    copies = [
        pltpu.make_async_copy(resist, resist_hbm, sems.at[0]),
        pltpu.make_async_copy(grad, grad_hbm, sems.at[1]),
    ]
    for copy in copies:
        copy.start()
    for copy in copies:
        copy.wait()


def shards(count, mask_params, target, kernel_spectra, kernel_weights):
    strip_rows, columns = mask_params.shape
    kernels, freq_rows, freq_cols = kernel_spectra.shape[1:]
    tables = make_tables(strip_rows, columns, freq_rows, freq_cols)
    names = list(tables)
    spectrum = (freq_rows, 2 * freq_cols)
    anywhere = pl.BlockSpec(memory_space=pl.ANY)
    out = jax.ShapeDtypeStruct((strip_rows, columns), jnp.float32)
    held = pltpu.VMEM((strip_rows, columns), jnp.float32)
    in_vmem = pl.BlockSpec(memory_space=pltpu.VMEM)
    resist, grad = pl.pallas_call(
        functools.partial(kernel, count, names),
        out_shape=(held, held),
        in_specs=[pl.BlockSpec(memory_space=pltpu.SMEM)] + [anywhere] * (3 + len(names)),
        out_specs=(in_vmem, in_vmem),
        scratch_shapes=[pltpu.VMEM(t.shape, jnp.bfloat16) for t in tables.values()]
        + [
            pltpu.VMEM((strip_rows, columns), jnp.float32),
            pltpu.VMEM((strip_rows, columns), jnp.int32),
            pltpu.VMEM(kernel_spectra.shape, jnp.float32),
            pltpu.VMEM((strip_rows, columns), jnp.float32),
            pltpu.VMEM((kernels // GROUP, 4 * freq_rows, GROUP * 2 * freq_cols), jnp.float32),
            pltpu.VMEM((2,) + spectrum, jnp.float32),
            pltpu.VMEM((2,) + spectrum, jnp.float32),
            pltpu.VMEM(spectrum, jnp.float32),
            pltpu.VMEM((2,) + spectrum, jnp.float32),
            pltpu.SemaphoreType.DMA((2 + 2 * CHUNKS + len(names),)),
            pltpu.SemaphoreType.DMA((4,)),
            pltpu.SemaphoreType.DMA((4,)),
        ],
        compiler_params=pltpu.CompilerParams(
            collective_id=0, has_side_effects=True, vmem_limit_bytes=56 * 1024 * 1024
        ),
        name="litho_step",
    )(kernel_weights, mask_params, target, kernel_spectra, *[jnp.asarray(t) for t in tables.values()])
    return pl.pallas_call(
        store,
        out_shape=(out, out),
        in_specs=[in_vmem, in_vmem],
        out_specs=(anywhere, anywhere),
        scratch_shapes=[pltpu.SemaphoreType.DMA((2,))],
        name="store_results",
    )(*[pltpu.with_memory_space_constraint(x, pltpu.VMEM) for x in (resist, grad)])


def solution(mesh):
    rows = P(("parts", "tiles"), None)
    body = functools.partial(shards, mesh.shape["tiles"])
    return jax.shard_map(
        body, mesh=mesh, in_specs=(rows, rows, P(), P()), out_specs=(rows, rows), check_vma=False
    )
```

```python
import functools
import math

import jax
import jax.numpy as jnp
import ml_dtypes
import numpy as np
from jax import lax
from jax.experimental import pallas as pl
from jax.experimental.pallas import tpu as pltpu
from jax.sharding import PartitionSpec as P

MARGIN = 64
STEEPNESS = 8.0
THRESHOLD = 0.35
GROUP = 4
CHUNKS = 4
MESH = pl.DeviceIdType.MESH


def split_table(table):
    high = table.astype(ml_dtypes.bfloat16)
    low = (table - high.astype(np.float64)).astype(ml_dtypes.bfloat16)
    return high, low


def deep_table(table):
    high, low = split_table(table)
    return np.concatenate([high, high, low], axis=1)


def tall_table(table):
    high, low = split_table(table)
    return np.concatenate(
        [np.concatenate([high, high], axis=1), np.concatenate([low, low], axis=1)], axis=0
    )


def long_table(table):
    high, low = split_table(table)
    return np.concatenate([high, high, low], axis=0)


def cos_sin(frequencies, positions):
    angles = 2.0 * math.pi * np.outer(frequencies, positions)
    return np.cos(angles), np.sin(angles)


def interpolation(half_band, coarse, fine_positions):
    degrees = np.arange(1, half_band)
    offsets = fine_positions[:, None] - (np.arange(coarse) / coarse)[None, :]
    waves = np.cos(2.0 * math.pi * offsets[:, :, None] * degrees).sum(axis=2)
    return (1.0 + 2.0 * waves) / coarse


def make_tables(strip_rows, columns, freq_rows, freq_cols):
    margin = MARGIN
    window = strip_rows + 2 * margin
    col_freq = np.arange(freq_cols) - freq_cols // 2
    row_freq = np.arange(freq_rows) - freq_rows // 2
    col_cos, col_sin = cos_sin(col_freq, np.arange(columns) / columns)
    row_cos, row_sin = cos_sin(row_freq, np.arange(window) / window)
    factor = 1.0 / math.sqrt(window * columns)
    forward = np.concatenate([col_cos.T, -col_sin.T], axis=1) * factor
    stack = np.concatenate([row_cos, row_sin], axis=0)
    own = stack[:, margin : margin + strip_rows]
    to_prev = np.zeros_like(own)
    to_prev[:, :margin] = stack[:, margin + strip_rows :]
    to_next = np.zeros_like(own)
    to_next[:, strip_rows - margin :] = stack[:, :margin]
    rows_in = np.concatenate([to_prev, to_next, own], axis=0)
    rows_near = np.concatenate([to_prev, to_next], axis=0).T
    coarse_rows, coarse_cols = 2 * freq_rows, 2 * freq_cols
    ccos, csin = cos_sin(col_freq, np.arange(coarse_cols) / coarse_cols)
    rcos, rsin = cos_sin(row_freq, np.arange(coarse_rows) / coarse_rows)
    inverse = np.concatenate(
        [np.concatenate([ccos, csin], axis=1), np.concatenate([-csin, ccos], axis=1)], axis=0
    )
    rows_out = np.concatenate(
        [np.concatenate([rcos.T, -rsin.T], axis=1), np.concatenate([rsin.T, rcos.T], axis=1)],
        axis=0,
    )
    own_positions = (margin + np.arange(strip_rows)) / window
    up_rows = interpolation(freq_rows, coarse_rows, own_positions)
    up_cols = interpolation(freq_cols, coarse_cols, np.arange(columns) / columns).T
    return {
        "forward": np.stack(split_table(forward)),
        "rows_in": deep_table(rows_in),
        "inverse": long_table(inverse),
        "rows_out": deep_table(rows_out),
        "up_cols": np.stack(split_table(up_cols)),
        "up_rows": deep_table(up_rows),
        "down_rows": tall_table(up_rows.T),
        "down_cols": np.stack(split_table(up_cols.T)),
        "rows_back": tall_table(rows_out.T),
        "inverse_back": long_table(inverse.T),
        "rows_own": deep_table(own.T),
        "rows_near": deep_table(rows_near),
        "forward_back": np.stack(split_table(forward.T)),
    }


def split(values):
    high = values.astype(jnp.bfloat16)
    low = (values - high.astype(jnp.float32)).astype(jnp.bfloat16)
    return high, low


def dot(left, right):
    return jnp.dot(left, right, preferred_element_type=jnp.float32)


def times_table(values, table, part=slice(None)):
    rows = values.shape[0]
    high, low = split(values)
    both = dot(jnp.concatenate([high, low], axis=0), table[0, part])
    return both[:rows] + (both[rows:] + dot(high, table[1, part]))


def table_times(deep, values):
    high, low = split(values)
    return dot(deep, jnp.concatenate([high, low, high], axis=0))


def times_long(values, long):
    high, low = split(values)
    return dot(jnp.concatenate([high, low, high], axis=1), long)


def tall_times(tall, values):
    product = dot(tall, jnp.concatenate(split(values), axis=0))
    half = product.shape[0] // 2
    return product[:half] + product[half:]


def fold(product):
    half_rows, half_cols = product.shape[0] // 2, product.shape[1] // 2
    real = product[:half_rows, :half_cols] + product[half_rows:, half_cols:]
    imag = product[:half_rows, half_cols:] - product[half_rows:, :half_cols]
    return jnp.concatenate([real, imag], axis=1)


def unfold(spectrum):
    half = spectrum.shape[1] // 2
    real, imag = spectrum[:, :half], spectrum[:, half:]
    return jnp.concatenate(
        [spectrum, jnp.concatenate([-imag, real], axis=1)], axis=0
    )


def kernel(count, names, weights_ref, mask_hbm, target_hbm, spectra_hbm, *refs):
    tables_hbm = refs[: len(names)]
    refs = refs[len(names) :]
    resist, grad = refs[:2]
    refs = refs[2:]
    tables = dict(zip(names, refs[: len(names)]))
    refs = refs[len(names) :]
    (mask, target, spectra, transmit, fields,
     send1, recv1, send2, recv2, in_sem, send_sem, recv_sem) = refs

    me = lax.axis_index("tiles")
    following = lax.rem(me + 1, count)
    previous = lax.rem(me + count - 1, count)
    barrier = pltpu.get_barrier_semaphore()
    for other in (previous, following):
        pl.semaphore_signal(barrier, inc=1, device_id={"tiles": other}, device_id_type=MESH)

    sources = {"spectra": (spectra_hbm, spectra), "target": (target_hbm, target)}
    for name, source in zip(names, tables_hbm):
        sources[name] = (source, tables[name])
    columns = mask.shape[1]
    chunks = CHUNKS if columns % (128 * CHUNKS) == 0 else 1
    parts = [pl.ds(at * (columns // chunks), columns // chunks) for at in range(chunks)]
    loads = {}

    def load(name, source, destination):
        loads[name] = pltpu.make_async_copy(source, destination, in_sem.at[len(loads)])
        loads[name].start()

    def table(name):
        loads[name].wait()
        return tables[name]

    for at, part in enumerate(parts):
        load(("mask", at), mask_hbm.at[:, part], mask.at[:, part])
        load(("forward", at), sources["forward"][0].at[:, part], tables["forward"].at[:, part])
    load("rows_in", *sources["rows_in"])

    def swap(step, to_previous, to_following):
        landed = recv1 if step == 0 else recv2
        copies = [
            pltpu.make_async_remote_copy(
                src_ref=to_following, dst_ref=landed.at[0],
                send_sem=send_sem.at[2 * step], recv_sem=recv_sem.at[2 * step],
                device_id={"tiles": following}, device_id_type=MESH),
            pltpu.make_async_remote_copy(
                src_ref=to_previous, dst_ref=landed.at[1],
                send_sem=send_sem.at[2 * step + 1], recv_sem=recv_sem.at[2 * step + 1],
                device_id={"tiles": previous}, device_id_type=MESH),
        ]
        for copy in copies:
            copy.start()
        return copies

    later = ("spectra", "inverse", "rows_out", "up_cols", "up_rows", "target", "down_rows",
             "down_cols", "rows_back", "inverse_back", "rows_own", "rows_near", "forward_back")

    column_spec = None
    for at, part in enumerate(parts):
        loads["mask", at].wait()
        transmit[:, part] = jnp.tanh(mask[:, part])
        loads["forward", at].wait()
        if at == len(parts) - 1:
            for name in later:
                load(name, *sources[name])
        term = times_table(transmit[:, part], tables["forward"], part)
        column_spec = term if column_spec is None else column_spec + term
    product = table_times(table("rows_in")[...], column_spec)
    span = product.shape[0] // 3
    send1[0] = fold(product[:span])
    send1[1] = fold(product[span : 2 * span])
    pl.semaphore_wait(barrier, 2)
    first_swap = swap(0, send1.at[0], send1.at[1])
    own_spec = fold(product[2 * span :])

    kernels, freq_rows, freq_cols = spectra.shape[1:]
    loads["spectra"].wait()
    weights = [jnp.full((1, freq_cols), weights_ref[k], jnp.float32) for k in range(kernels)]
    total = functools.reduce(jnp.add, weights)
    for k in range(kernels):
        scale = jnp.sqrt(weights[k] / total)
        spectra[0, k] = spectra[0, k] * scale
        spectra[1, k] = spectra[1, k] * scale
    inverse, rows_out = table("inverse"), table("rows_out")

    for copy in first_swap:
        copy.wait_recv()
    spec = own_spec + (recv1[0] + recv1[1])
    spec_real, spec_imag = spec[:, :freq_cols], spec[:, freq_cols:]

    coarse = fields.shape[1] // 2
    width = fields.shape[2] // GROUP

    def add_fields(group, power):
        blocks = []
        for place in range(GROUP):
            k = group * GROUP + place
            real = spectra[0, k] * spec_real - spectra[1, k] * spec_imag
            imag = spectra[0, k] * spec_imag + spectra[1, k] * spec_real
            blocks.append(jnp.concatenate([real, imag], axis=1))
        across = times_long(jnp.concatenate(blocks, axis=0), inverse[...])
        blocks = []
        for place in range(GROUP):
            part = across[place * freq_rows : (place + 1) * freq_rows]
            blocks.append(jnp.concatenate([part[:, :width], part[:, width:]], axis=0))
        field = table_times(rows_out[...], jnp.concatenate(blocks, axis=1))
        fields[group] = field
        terms = field[:coarse] * field[:coarse] + field[coarse:] * field[coarse:]
        for place in range(GROUP):
            power = power + terms[:, place * width : (place + 1) * width]
        return power

    groups = fields.shape[0]
    power = lax.fori_loop(0, groups, add_fields, jnp.zeros((coarse, width), jnp.float32))

    intensity = table_times(table("up_rows")[...], times_table(power, table("up_cols")))
    image = jax.nn.sigmoid(STEEPNESS * (intensity - THRESHOLD))
    resist[...] = image
    loads["target"].wait()
    slopes = (4.0 * STEEPNESS) * (image - target[...].astype(jnp.float32)) * image * (1.0 - image)
    slopes = times_table(tall_times(table("down_rows")[...], slopes), table("down_cols"))
    slopes = jnp.concatenate([slopes, slopes], axis=0)
    slopes = jnp.concatenate([slopes] * GROUP, axis=1)

    rows_back, inverse_back = table("rows_back"), table("inverse_back")

    def add_gradient(group, sums):
        grad_real, grad_imag = sums
        part = tall_times(rows_back[...], fields[group] * slopes)
        blocks = []
        for place in range(GROUP):
            piece = part[:, place * width : (place + 1) * width]
            blocks.append(jnp.concatenate([piece[:freq_rows], piece[freq_rows:]], axis=1))
        across = times_long(jnp.concatenate(blocks, axis=0), inverse_back[...])
        for place in range(GROUP):
            k = group * GROUP + place
            part = across[place * freq_rows : (place + 1) * freq_rows]
            real, imag = part[:, :freq_cols], part[:, freq_cols:]
            grad_real = grad_real + (real * spectra[0, k] + imag * spectra[1, k])
            grad_imag = grad_imag + (imag * spectra[0, k] - real * spectra[1, k])
        return grad_real, grad_imag

    empty = jnp.zeros((freq_rows, freq_cols), jnp.float32)
    grad_real, grad_imag = lax.fori_loop(0, groups, add_gradient, (empty, empty))
    window_grad = jnp.concatenate([grad_real, grad_imag], axis=1)
    send2[...] = window_grad
    second_swap = swap(1, send2, send2)
    merged = table_times(table("rows_own")[...], unfold(window_grad))
    rows_near, forward_back = table("rows_near"), table("forward_back")
    for copy in second_swap:
        copy.wait_recv()
    near = jnp.concatenate([unfold(recv2[0]), unfold(recv2[1])], axis=0)
    merged = merged + table_times(rows_near[...], near)
    held = transmit[...]
    grad[...] = times_table(merged, forward_back) * (1.0 - held * held)
    for copy in first_swap + second_swap:
        copy.wait_send()


def store(resist, grad, resist_hbm, grad_hbm, sems):
    copies = [
        pltpu.make_async_copy(resist, resist_hbm, sems.at[0]),
        pltpu.make_async_copy(grad, grad_hbm, sems.at[1]),
    ]
    for copy in copies:
        copy.start()
    for copy in copies:
        copy.wait()


def shards(count, mask_params, target, kernel_spectra, kernel_weights):
    strip_rows, columns = mask_params.shape
    kernels, freq_rows, freq_cols = kernel_spectra.shape[1:]
    tables = make_tables(strip_rows, columns, freq_rows, freq_cols)
    names = list(tables)
    spectrum = (freq_rows, 2 * freq_cols)
    anywhere = pl.BlockSpec(memory_space=pl.ANY)
    out = jax.ShapeDtypeStruct((strip_rows, columns), jnp.float32)
    held = pltpu.VMEM((strip_rows, columns), jnp.float32)
    in_vmem = pl.BlockSpec(memory_space=pltpu.VMEM)
    resist, grad = pl.pallas_call(
        functools.partial(kernel, count, names),
        out_shape=(held, held),
        in_specs=[pl.BlockSpec(memory_space=pltpu.SMEM)] + [anywhere] * (3 + len(names)),
        out_specs=(in_vmem, in_vmem),
        scratch_shapes=[pltpu.VMEM(t.shape, jnp.bfloat16) for t in tables.values()]
        + [
            pltpu.VMEM((strip_rows, columns), jnp.float32),
            pltpu.VMEM((strip_rows, columns), jnp.int32),
            pltpu.VMEM(kernel_spectra.shape, jnp.float32),
            pltpu.VMEM((strip_rows, columns), jnp.float32),
            pltpu.VMEM((kernels // GROUP, 4 * freq_rows, GROUP * 2 * freq_cols), jnp.float32),
            pltpu.VMEM((2,) + spectrum, jnp.float32),
            pltpu.VMEM((2,) + spectrum, jnp.float32),
            pltpu.VMEM(spectrum, jnp.float32),
            pltpu.VMEM((2,) + spectrum, jnp.float32),
            pltpu.SemaphoreType.DMA((2 + 2 * CHUNKS + len(names),)),
            pltpu.SemaphoreType.DMA((4,)),
            pltpu.SemaphoreType.DMA((4,)),
        ],
        compiler_params=pltpu.CompilerParams(
            collective_id=0, has_side_effects=True, vmem_limit_bytes=56 * 1024 * 1024
        ),
        name="litho_step",
    )(kernel_weights, mask_params, target, kernel_spectra, *[jnp.asarray(t) for t in tables.values()])
    return pl.pallas_call(
        store,
        out_shape=(out, out),
        in_specs=[in_vmem, in_vmem],
        out_specs=(anywhere, anywhere),
        scratch_shapes=[pltpu.SemaphoreType.DMA((2,))],
        name="store_results",
    )(*[pltpu.with_memory_space_constraint(x, pltpu.VMEM) for x in (resist, grad)])


def solution(mesh):
    rows = P(("parts", "tiles"), None)
    body = functools.partial(shards, mesh.shape["tiles"])
    return jax.shard_map(
        body, mesh=mesh, in_specs=(rows, rows, P(), P()), out_specs=(rows, rows), check_vma=False
    )
```

```python
import functools
import math

import jax
import jax.numpy as jnp
import ml_dtypes
import numpy as np
from jax import lax
from jax.experimental import pallas as pl
from jax.experimental.pallas import tpu as pltpu
from jax.sharding import PartitionSpec as P

MARGIN = 64
STEEPNESS = 8.0
THRESHOLD = 0.35
GROUP = 4
CHUNKS = 4
MESH = pl.DeviceIdType.MESH


def split_table(table):
    high = table.astype(ml_dtypes.bfloat16)
    low = (table - high.astype(np.float64)).astype(ml_dtypes.bfloat16)
    return high, low


def deep_table(table):
    high, low = split_table(table)
    return np.concatenate([high, high, low], axis=1)


def tall_table(table):
    high, low = split_table(table)
    return np.concatenate(
        [np.concatenate([high, high], axis=1), np.concatenate([low, low], axis=1)], axis=0
    )


def long_table(table):
    high, low = split_table(table)
    return np.concatenate([high, high, low], axis=0)


def cos_sin(frequencies, positions):
    angles = 2.0 * math.pi * np.outer(frequencies, positions)
    return np.cos(angles), np.sin(angles)


def interpolation(half_band, coarse, fine_positions):
    degrees = np.arange(1, half_band)
    offsets = fine_positions[:, None] - (np.arange(coarse) / coarse)[None, :]
    waves = np.cos(2.0 * math.pi * offsets[:, :, None] * degrees).sum(axis=2)
    return (1.0 + 2.0 * waves) / coarse


def make_tables(strip_rows, columns, freq_rows, freq_cols):
    margin = MARGIN
    window = strip_rows + 2 * margin
    col_freq = np.arange(freq_cols) - freq_cols // 2
    row_freq = np.arange(freq_rows) - freq_rows // 2
    col_cos, col_sin = cos_sin(col_freq, np.arange(columns) / columns)
    row_cos, row_sin = cos_sin(row_freq, np.arange(window) / window)
    factor = 1.0 / math.sqrt(window * columns)
    forward = np.concatenate([col_cos.T, -col_sin.T], axis=1) * factor
    stack = np.concatenate([row_cos, row_sin], axis=0)
    own = stack[:, margin : margin + strip_rows]
    to_prev = np.zeros_like(own)
    to_prev[:, :margin] = stack[:, margin + strip_rows :]
    to_next = np.zeros_like(own)
    to_next[:, strip_rows - margin :] = stack[:, :margin]
    rows_in = np.concatenate([to_prev, to_next, own], axis=0)
    rows_near = np.concatenate([to_prev, to_next], axis=0).T
    coarse_rows, coarse_cols = 2 * freq_rows, 2 * freq_cols
    ccos, csin = cos_sin(col_freq, np.arange(coarse_cols) / coarse_cols)
    rcos, rsin = cos_sin(row_freq, np.arange(coarse_rows) / coarse_rows)
    inverse = np.concatenate(
        [np.concatenate([ccos, csin], axis=1), np.concatenate([-csin, ccos], axis=1)], axis=0
    )
    rows_out = np.concatenate(
        [np.concatenate([rcos.T, -rsin.T], axis=1), np.concatenate([rsin.T, rcos.T], axis=1)],
        axis=0,
    )
    own_positions = (margin + np.arange(strip_rows)) / window
    up_rows = interpolation(freq_rows, coarse_rows, own_positions)
    up_cols = interpolation(freq_cols, coarse_cols, np.arange(columns) / columns).T
    return {
        "forward": np.stack(split_table(forward)),
        "rows_in": deep_table(rows_in),
        "inverse": long_table(inverse),
        "rows_out": deep_table(rows_out),
        "up_cols": np.stack(split_table(up_cols)),
        "up_rows": deep_table(up_rows),
        "down_rows": tall_table(up_rows.T),
        "down_cols": np.stack(split_table(up_cols.T)),
        "rows_back": tall_table(rows_out.T),
        "inverse_back": long_table(inverse.T),
        "rows_own": deep_table(own.T),
        "rows_near": deep_table(rows_near),
        "forward_back": np.stack(split_table(forward.T)),
    }


def split(values):
    high = values.astype(jnp.bfloat16)
    low = (values - high.astype(jnp.float32)).astype(jnp.bfloat16)
    return high, low


def dot(left, right):
    return jnp.dot(left, right, preferred_element_type=jnp.float32)


def times_table(values, table, part=slice(None)):
    rows = values.shape[0]
    high, low = split(values)
    both = dot(jnp.concatenate([high, low], axis=0), table[0, part])
    return both[:rows] + (both[rows:] + dot(high, table[1, part]))


def table_times(deep, values):
    high, low = split(values)
    return dot(deep, jnp.concatenate([high, low, high], axis=0))


def times_long(values, long):
    high, low = split(values)
    return dot(jnp.concatenate([high, low, high], axis=1), long)


def tall_times(tall, values):
    product = dot(tall, jnp.concatenate(split(values), axis=0))
    half = product.shape[0] // 2
    return product[:half] + product[half:]


def fold(product):
    half_rows, half_cols = product.shape[0] // 2, product.shape[1] // 2
    real = product[:half_rows, :half_cols] + product[half_rows:, half_cols:]
    imag = product[:half_rows, half_cols:] - product[half_rows:, :half_cols]
    return jnp.concatenate([real, imag], axis=1)


def unfold(spectrum):
    half = spectrum.shape[1] // 2
    real, imag = spectrum[:, :half], spectrum[:, half:]
    return jnp.concatenate(
        [spectrum, jnp.concatenate([-imag, real], axis=1)], axis=0
    )


def kernel(count, names, weights_ref, mask_hbm, target_hbm, spectra_hbm, *refs):
    tables_hbm = refs[: len(names)]
    refs = refs[len(names) :]
    resist, merged_ref, transmit, last_table = refs[:4]
    refs = refs[4:]
    held = [name for name in names if name != "forward_back"]
    tables = dict(zip(held, refs[: len(held)]), forward_back=last_table)
    refs = refs[len(held) :]
    (mask, target, spectra, fields,
     send1, recv1, send2, recv2, in_sem, send_sem, recv_sem) = refs

    me = lax.axis_index("tiles")
    following = lax.rem(me + 1, count)
    previous = lax.rem(me + count - 1, count)
    barrier = pltpu.get_barrier_semaphore()
    for other in (previous, following):
        pl.semaphore_signal(barrier, inc=1, device_id={"tiles": other}, device_id_type=MESH)

    sources = {"spectra": (spectra_hbm, spectra), "target": (target_hbm, target)}
    for name, source in zip(names, tables_hbm):
        sources[name] = (source, tables[name])
    columns = mask.shape[1]
    chunks = CHUNKS if columns % (128 * CHUNKS) == 0 else 1
    parts = [pl.ds(at * (columns // chunks), columns // chunks) for at in range(chunks)]
    loads = {}

    def load(name, source, destination):
        loads[name] = pltpu.make_async_copy(source, destination, in_sem.at[len(loads)])
        loads[name].start()

    def table(name):
        loads[name].wait()
        return tables[name]

    for at, part in enumerate(parts):
        load(("mask", at), mask_hbm.at[:, part], mask.at[:, part])
        load(("forward", at), sources["forward"][0].at[:, part], tables["forward"].at[:, part])
    load("rows_in", *sources["rows_in"])

    def swap(step, to_previous, to_following):
        landed = recv1 if step == 0 else recv2
        copies = [
            pltpu.make_async_remote_copy(
                src_ref=to_following, dst_ref=landed.at[0],
                send_sem=send_sem.at[2 * step], recv_sem=recv_sem.at[2 * step],
                device_id={"tiles": following}, device_id_type=MESH),
            pltpu.make_async_remote_copy(
                src_ref=to_previous, dst_ref=landed.at[1],
                send_sem=send_sem.at[2 * step + 1], recv_sem=recv_sem.at[2 * step + 1],
                device_id={"tiles": previous}, device_id_type=MESH),
        ]
        for copy in copies:
            copy.start()
        return copies

    later = ("spectra", "inverse", "rows_out", "up_cols", "up_rows", "target", "down_rows",
             "down_cols", "rows_back", "inverse_back", "rows_own", "rows_near", "forward_back")

    column_spec = None
    for at, part in enumerate(parts):
        loads["mask", at].wait()
        transmit[:, part] = jnp.tanh(mask[:, part])
        loads["forward", at].wait()
        if at == len(parts) - 1:
            for name in later:
                load(name, *sources[name])
        term = times_table(transmit[:, part], tables["forward"], part)
        column_spec = term if column_spec is None else column_spec + term
    product = table_times(table("rows_in")[...], column_spec)
    span = product.shape[0] // 3
    send1[0] = fold(product[:span])
    send1[1] = fold(product[span : 2 * span])
    pl.semaphore_wait(barrier, 2)
    first_swap = swap(0, send1.at[0], send1.at[1])
    own_spec = fold(product[2 * span :])

    kernels, freq_rows, freq_cols = spectra.shape[1:]
    loads["spectra"].wait()
    weights = [jnp.full((1, freq_cols), weights_ref[k], jnp.float32) for k in range(kernels)]
    total = functools.reduce(jnp.add, weights)
    for k in range(kernels):
        scale = jnp.sqrt(weights[k] / total)
        spectra[0, k] = spectra[0, k] * scale
        spectra[1, k] = spectra[1, k] * scale
    inverse, rows_out = table("inverse"), table("rows_out")

    for copy in first_swap:
        copy.wait_recv()
    spec = own_spec + (recv1[0] + recv1[1])
    spec_real, spec_imag = spec[:, :freq_cols], spec[:, freq_cols:]

    coarse = fields.shape[1] // 2
    width = fields.shape[2] // GROUP
    blocks = []
    for k in range(kernels):
        real = spectra[0, k] * spec_real - spectra[1, k] * spec_imag
        imag = spectra[0, k] * spec_imag + spectra[1, k] * spec_real
        blocks.append(jnp.concatenate([real, imag], axis=1))
    across = times_long(jnp.concatenate(blocks, axis=0), inverse[...])
    power = None
    for group in range(fields.shape[0]):
        blocks = []
        for k in range(group * GROUP, (group + 1) * GROUP):
            part = across[k * freq_rows : (k + 1) * freq_rows]
            blocks.append(jnp.concatenate([part[:, :width], part[:, width:]], axis=0))
        field = table_times(rows_out[...], jnp.concatenate(blocks, axis=1))
        fields[group] = field
        terms = field[:coarse] * field[:coarse] + field[coarse:] * field[coarse:]
        for place in range(GROUP):
            term = terms[:, place * width : (place + 1) * width]
            power = term if power is None else power + term

    intensity = table_times(table("up_rows")[...], times_table(power, table("up_cols")))
    image = jax.nn.sigmoid(STEEPNESS * (intensity - THRESHOLD))
    resist[...] = image
    loads["target"].wait()
    slopes = (4.0 * STEEPNESS) * (image - target[...].astype(jnp.float32)) * image * (1.0 - image)
    slopes = times_table(tall_times(table("down_rows")[...], slopes), table("down_cols"))
    slopes = jnp.concatenate([slopes, slopes], axis=0)
    slopes = jnp.concatenate([slopes] * GROUP, axis=1)

    rows_back, inverse_back = table("rows_back"), table("inverse_back")
    blocks = []
    for group in range(fields.shape[0]):
        part = tall_times(rows_back[...], fields[group] * slopes)
        for place in range(GROUP):
            piece = part[:, place * width : (place + 1) * width]
            blocks.append(jnp.concatenate([piece[:freq_rows], piece[freq_rows:]], axis=1))
    across = times_long(jnp.concatenate(blocks, axis=0), inverse_back[...])
    grad_real = grad_imag = None
    for k in range(kernels):
        part = across[k * freq_rows : (k + 1) * freq_rows]
        real, imag = part[:, :freq_cols], part[:, freq_cols:]
        term_real = real * spectra[0, k] + imag * spectra[1, k]
        term_imag = imag * spectra[0, k] - real * spectra[1, k]
        grad_real = term_real if grad_real is None else grad_real + term_real
        grad_imag = term_imag if grad_imag is None else grad_imag + term_imag
    window_grad = jnp.concatenate([grad_real, grad_imag], axis=1)
    send2[...] = window_grad
    second_swap = swap(1, send2, send2)
    merged = table_times(table("rows_own")[...], unfold(window_grad))
    rows_near = table("rows_near")
    loads["forward_back"].wait()
    for copy in second_swap:
        copy.wait_recv()
    near = jnp.concatenate([unfold(recv2[0]), unfold(recv2[1])], axis=0)
    merged_ref[...] = merged + table_times(rows_near[...], near)
    for copy in first_swap + second_swap:
        copy.wait_send()


def finish(resist, merged, transmit, table, resist_hbm, grad_hbm, grad, sems):
    copies = [pltpu.make_async_copy(resist, resist_hbm, sems.at[0])]
    copies[0].start()
    rows, columns = grad.shape
    chunks = CHUNKS if columns % (128 * CHUNKS) == 0 else 1
    high, low = split(merged[...])
    left = jnp.concatenate([high, low], axis=0)
    for at in range(chunks):
        part = pl.ds(at * (columns // chunks), columns // chunks)
        both = dot(left, table[0, :, part])
        product = both[:rows] + (both[rows:] + dot(high, table[1, :, part]))
        held = transmit[:, part]
        grad[:, part] = product * (1.0 - held * held)
        copy = pltpu.make_async_copy(grad.at[:, part], grad_hbm.at[:, part], sems.at[1 + at])
        copy.start()
        copies.append(copy)
    for copy in copies:
        copy.wait()


def shards(count, mask_params, target, kernel_spectra, kernel_weights):
    strip_rows, columns = mask_params.shape
    kernels, freq_rows, freq_cols = kernel_spectra.shape[1:]
    tables = make_tables(strip_rows, columns, freq_rows, freq_cols)
    names = list(tables)
    spectrum = (freq_rows, 2 * freq_cols)
    anywhere = pl.BlockSpec(memory_space=pl.ANY)
    out = jax.ShapeDtypeStruct((strip_rows, columns), jnp.float32)
    held = pltpu.VMEM((strip_rows, columns), jnp.float32)
    in_vmem = pl.BlockSpec(memory_space=pltpu.VMEM)
    merged = pltpu.VMEM((strip_rows, 2 * freq_cols), jnp.float32)
    last = pltpu.VMEM(tables["forward_back"].shape, jnp.bfloat16)
    results = pl.pallas_call(
        functools.partial(kernel, count, names),
        out_shape=(held, merged, held, last),
        in_specs=[pl.BlockSpec(memory_space=pltpu.SMEM)] + [anywhere] * (3 + len(names)),
        out_specs=(in_vmem,) * 4,
        scratch_shapes=[pltpu.VMEM(tables[n].shape, jnp.bfloat16) for n in names if n != "forward_back"]
        + [
            pltpu.VMEM((strip_rows, columns), jnp.float32),
            pltpu.VMEM((strip_rows, columns), jnp.int32),
            pltpu.VMEM(kernel_spectra.shape, jnp.float32),
            pltpu.VMEM((kernels // GROUP, 4 * freq_rows, GROUP * 2 * freq_cols), jnp.float32),
            pltpu.VMEM((2,) + spectrum, jnp.float32),
            pltpu.VMEM((2,) + spectrum, jnp.float32),
            pltpu.VMEM(spectrum, jnp.float32),
            pltpu.VMEM((2,) + spectrum, jnp.float32),
            pltpu.SemaphoreType.DMA((2 + 2 * CHUNKS + len(names),)),
            pltpu.SemaphoreType.DMA((4,)),
            pltpu.SemaphoreType.DMA((4,)),
        ],
        compiler_params=pltpu.CompilerParams(
            collective_id=0, has_side_effects=True, vmem_limit_bytes=56 * 1024 * 1024
        ),
        name="litho_step",
    )(kernel_weights, mask_params, target, kernel_spectra, *[jnp.asarray(t) for t in tables.values()])
    return pl.pallas_call(
        finish,
        out_shape=(out, out),
        in_specs=[in_vmem] * 4,
        out_specs=(anywhere, anywhere),
        scratch_shapes=[
            pltpu.VMEM((strip_rows, columns), jnp.float32),
            pltpu.SemaphoreType.DMA((1 + CHUNKS,)),
        ],
        compiler_params=pltpu.CompilerParams(vmem_limit_bytes=32 * 1024 * 1024),
        name="finish_gradient",
    )(*[pltpu.with_memory_space_constraint(x, pltpu.VMEM) for x in results])


def solution(mesh):
    rows = P(("parts", "tiles"), None)
    body = functools.partial(shards, mesh.shape["tiles"])
    return jax.shard_map(
        body, mesh=mesh, in_specs=(rows, rows, P(), P()), out_specs=(rows, rows), check_vma=False
    )
```

```python
import functools
import math

import jax
import jax.numpy as jnp
import ml_dtypes
import numpy as np
from jax import lax
from jax.experimental import pallas as pl
from jax.experimental.pallas import tpu as pltpu
from jax.sharding import PartitionSpec as P

MARGIN = 64
STEEPNESS = 8.0
THRESHOLD = 0.35
GROUP = 4
BATCH = 8
CHUNKS = 4
MESH = pl.DeviceIdType.MESH


def split_table(table):
    high = table.astype(ml_dtypes.bfloat16)
    low = (table - high.astype(np.float64)).astype(ml_dtypes.bfloat16)
    return high, low


def deep_table(table):
    high, low = split_table(table)
    return np.concatenate([high, high, low], axis=1)


def tall_table(table):
    high, low = split_table(table)
    return np.concatenate(
        [np.concatenate([high, high], axis=1), np.concatenate([low, low], axis=1)], axis=0
    )


def long_table(table):
    high, low = split_table(table)
    return np.concatenate([high, high, low], axis=0)


def cos_sin(frequencies, positions):
    angles = 2.0 * math.pi * np.outer(frequencies, positions)
    return np.cos(angles), np.sin(angles)


def interpolation(half_band, coarse, fine_positions):
    degrees = np.arange(1, half_band)
    offsets = fine_positions[:, None] - (np.arange(coarse) / coarse)[None, :]
    waves = np.cos(2.0 * math.pi * offsets[:, :, None] * degrees).sum(axis=2)
    return (1.0 + 2.0 * waves) / coarse


def make_tables(strip_rows, columns, freq_rows, freq_cols):
    margin = MARGIN
    window = strip_rows + 2 * margin
    col_freq = np.arange(freq_cols) - freq_cols // 2
    row_freq = np.arange(freq_rows) - freq_rows // 2
    col_cos, col_sin = cos_sin(col_freq, np.arange(columns) / columns)
    row_cos, row_sin = cos_sin(row_freq, np.arange(window) / window)
    factor = 1.0 / math.sqrt(window * columns)
    forward = np.concatenate([col_cos.T, -col_sin.T], axis=1) * factor
    stack = np.concatenate([row_cos, row_sin], axis=0)
    own = stack[:, margin : margin + strip_rows]
    to_prev = np.zeros_like(own)
    to_prev[:, :margin] = stack[:, margin + strip_rows :]
    to_next = np.zeros_like(own)
    to_next[:, strip_rows - margin :] = stack[:, :margin]
    rows_in = np.concatenate([to_prev, to_next, own], axis=0)
    rows_near = np.concatenate([to_prev, to_next], axis=0).T
    coarse_rows, coarse_cols = 2 * freq_rows, 2 * freq_cols
    ccos, csin = cos_sin(col_freq, np.arange(coarse_cols) / coarse_cols)
    rcos, rsin = cos_sin(row_freq, np.arange(coarse_rows) / coarse_rows)
    inverse = np.concatenate(
        [np.concatenate([ccos, csin], axis=1), np.concatenate([-csin, ccos], axis=1)], axis=0
    )
    rows_out = np.concatenate(
        [np.concatenate([rcos.T, -rsin.T], axis=1), np.concatenate([rsin.T, rcos.T], axis=1)],
        axis=0,
    )
    own_positions = (margin + np.arange(strip_rows)) / window
    up_rows = interpolation(freq_rows, coarse_rows, own_positions)
    up_cols = interpolation(freq_cols, coarse_cols, np.arange(columns) / columns).T
    return {
        "forward": np.stack(split_table(forward)),
        "rows_in": deep_table(rows_in),
        "inverse": long_table(inverse),
        "rows_out": deep_table(rows_out),
        "up_cols": np.stack(split_table(up_cols)),
        "up_rows": deep_table(up_rows),
        "down_rows": tall_table(up_rows.T),
        "down_cols": np.stack(split_table(up_cols.T)),
        "rows_back": tall_table(rows_out.T),
        "inverse_back": long_table(inverse.T),
        "rows_own": deep_table(own.T),
        "rows_near": deep_table(rows_near),
        "forward_back": np.stack(split_table(forward.T)),
    }


def split(values):
    high = values.astype(jnp.bfloat16)
    low = (values - high.astype(jnp.float32)).astype(jnp.bfloat16)
    return high, low


def dot(left, right):
    return jnp.dot(left, right, preferred_element_type=jnp.float32)


def times_table(values, table, part=slice(None)):
    rows = values.shape[0]
    high, low = split(values)
    both = dot(jnp.concatenate([high, low], axis=0), table[0, part])
    return both[:rows] + (both[rows:] + dot(high, table[1, part]))


def table_times(deep, values):
    high, low = split(values)
    return dot(deep, jnp.concatenate([high, low, high], axis=0))


def times_long(values, long):
    high, low = split(values)
    return dot(jnp.concatenate([high, low, high], axis=1), long)


def tall_times(tall, values):
    product = dot(tall, jnp.concatenate(split(values), axis=0))
    half = product.shape[0] // 2
    return product[:half] + product[half:]


def fold(product):
    half_rows, half_cols = product.shape[0] // 2, product.shape[1] // 2
    real = product[:half_rows, :half_cols] + product[half_rows:, half_cols:]
    imag = product[:half_rows, half_cols:] - product[half_rows:, :half_cols]
    return jnp.concatenate([real, imag], axis=1)


def unfold(spectrum):
    half = spectrum.shape[1] // 2
    real, imag = spectrum[:, :half], spectrum[:, half:]
    return jnp.concatenate(
        [spectrum, jnp.concatenate([-imag, real], axis=1)], axis=0
    )


def kernel(count, names, weights_ref, mask_hbm, target_hbm, spectra_hbm, *refs):
    tables_hbm = refs[: len(names)]
    refs = refs[len(names) :]
    resist, merged_ref, transmit, last_table = refs[:4]
    refs = refs[4:]
    held = [name for name in names if name != "forward_back"]
    tables = dict(zip(held, refs[: len(held)]), forward_back=last_table)
    refs = refs[len(held) :]
    (mask, target, spectra, fields,
     send1, recv1, send2, recv2, in_sem, send_sem, recv_sem) = refs

    me = lax.axis_index("tiles")
    following = lax.rem(me + 1, count)
    previous = lax.rem(me + count - 1, count)
    barrier = pltpu.get_barrier_semaphore()
    for other in (previous, following):
        pl.semaphore_signal(barrier, inc=1, device_id={"tiles": other}, device_id_type=MESH)

    sources = {"spectra": (spectra_hbm, spectra), "target": (target_hbm, target)}
    for name, source in zip(names, tables_hbm):
        sources[name] = (source, tables[name])
    columns = mask.shape[1]
    chunks = CHUNKS if columns % (128 * CHUNKS) == 0 else 1
    parts = [pl.ds(at * (columns // chunks), columns // chunks) for at in range(chunks)]
    loads = {}

    def load(name, source, destination):
        loads[name] = pltpu.make_async_copy(source, destination, in_sem.at[len(loads)])
        loads[name].start()

    def table(name):
        loads[name].wait()
        return tables[name]

    for at, part in enumerate(parts):
        load(("mask", at), mask_hbm.at[:, part], mask.at[:, part])
        load(("forward", at), sources["forward"][0].at[:, part], tables["forward"].at[:, part])
    load("rows_in", *sources["rows_in"])

    def swap(step, to_previous, to_following):
        landed = recv1 if step == 0 else recv2
        copies = [
            pltpu.make_async_remote_copy(
                src_ref=to_following, dst_ref=landed.at[0],
                send_sem=send_sem.at[2 * step], recv_sem=recv_sem.at[2 * step],
                device_id={"tiles": following}, device_id_type=MESH),
            pltpu.make_async_remote_copy(
                src_ref=to_previous, dst_ref=landed.at[1],
                send_sem=send_sem.at[2 * step + 1], recv_sem=recv_sem.at[2 * step + 1],
                device_id={"tiles": previous}, device_id_type=MESH),
        ]
        for copy in copies:
            copy.start()
        return copies

    later = ("spectra", "inverse", "rows_out", "up_cols", "up_rows", "target", "down_rows",
             "down_cols", "rows_back", "inverse_back", "rows_own", "rows_near", "forward_back")

    column_spec = None
    for at, part in enumerate(parts):
        loads["mask", at].wait()
        transmit[:, part] = jnp.tanh(mask[:, part])
        loads["forward", at].wait()
        if at == len(parts) - 1:
            for name in later:
                load(name, *sources[name])
        term = times_table(transmit[:, part], tables["forward"], part)
        column_spec = term if column_spec is None else column_spec + term
    product = table_times(table("rows_in")[...], column_spec)
    span = product.shape[0] // 3
    send1[0] = fold(product[:span])
    send1[1] = fold(product[span : 2 * span])
    pl.semaphore_wait(barrier, 2)
    first_swap = swap(0, send1.at[0], send1.at[1])
    own_spec = fold(product[2 * span :])

    kernels, freq_rows, freq_cols = spectra.shape[1:]
    loads["spectra"].wait()
    weights = [jnp.full((1, freq_cols), weights_ref[k], jnp.float32) for k in range(kernels)]
    total = functools.reduce(jnp.add, weights)
    for k in range(kernels):
        scale = jnp.sqrt(weights[k] / total)
        spectra[0, k] = spectra[0, k] * scale
        spectra[1, k] = spectra[1, k] * scale
    inverse, rows_out = table("inverse"), table("rows_out")

    for copy in first_swap:
        copy.wait_recv()
    spec = own_spec + (recv1[0] + recv1[1])
    spec_real, spec_imag = spec[:, :freq_cols], spec[:, freq_cols:]

    coarse = fields.shape[1] // 2
    width = fields.shape[2] // GROUP
    across = []
    for first in range(0, kernels, BATCH):
        blocks = []
        for k in range(first, min(first + BATCH, kernels)):
            real = spectra[0, k] * spec_real - spectra[1, k] * spec_imag
            imag = spectra[0, k] * spec_imag + spectra[1, k] * spec_real
            blocks.append(jnp.concatenate([real, imag], axis=1))
        across.append(times_long(jnp.concatenate(blocks, axis=0), inverse[...]))
    power = None
    for group in range(fields.shape[0]):
        blocks = []
        for k in range(group * GROUP, (group + 1) * GROUP):
            at = (k % BATCH) * freq_rows
            part = across[k // BATCH][at : at + freq_rows]
            blocks.append(jnp.concatenate([part[:, :width], part[:, width:]], axis=0))
        field = table_times(rows_out[...], jnp.concatenate(blocks, axis=1))
        fields[group] = field
        terms = field[:coarse] * field[:coarse] + field[coarse:] * field[coarse:]
        for place in range(GROUP):
            term = terms[:, place * width : (place + 1) * width]
            power = term if power is None else power + term

    intensity = table_times(table("up_rows")[...], times_table(power, table("up_cols")))
    image = 0.5 + 0.5 * jnp.tanh((0.5 * STEEPNESS) * (intensity - THRESHOLD))
    resist[...] = image
    loads["target"].wait()
    slopes = (4.0 * STEEPNESS) * (image - target[...].astype(jnp.float32)) * image * (1.0 - image)
    slopes = times_table(tall_times(table("down_rows")[...], slopes), table("down_cols"))
    slopes = jnp.concatenate([slopes, slopes], axis=0)
    slopes = jnp.concatenate([slopes] * GROUP, axis=1)

    rows_back, inverse_back = table("rows_back"), table("inverse_back")
    blocks = []
    for group in range(fields.shape[0]):
        part = tall_times(rows_back[...], fields[group] * slopes)
        for place in range(GROUP):
            piece = part[:, place * width : (place + 1) * width]
            blocks.append(jnp.concatenate([piece[:freq_rows], piece[freq_rows:]], axis=1))
    across = [
        times_long(jnp.concatenate(blocks[first : first + BATCH], axis=0), inverse_back[...])
        for first in range(0, kernels, BATCH)
    ]
    grad_real = grad_imag = None
    for k in range(kernels):
        at = (k % BATCH) * freq_rows
        part = across[k // BATCH][at : at + freq_rows]
        real, imag = part[:, :freq_cols], part[:, freq_cols:]
        term_real = real * spectra[0, k] + imag * spectra[1, k]
        term_imag = imag * spectra[0, k] - real * spectra[1, k]
        grad_real = term_real if grad_real is None else grad_real + term_real
        grad_imag = term_imag if grad_imag is None else grad_imag + term_imag
    window_grad = jnp.concatenate([grad_real, grad_imag], axis=1)
    send2[...] = window_grad
    second_swap = swap(1, send2, send2)
    merged = table_times(table("rows_own")[...], unfold(window_grad))
    rows_near = table("rows_near")
    loads["forward_back"].wait()
    for copy in second_swap:
        copy.wait_recv()
    near = jnp.concatenate([unfold(recv2[0]), unfold(recv2[1])], axis=0)
    merged_ref[...] = merged + table_times(rows_near[...], near)
    for copy in first_swap + second_swap:
        copy.wait_send()


def finish(resist, merged, transmit, table, resist_hbm, grad_hbm, grad, sems):
    copies = [pltpu.make_async_copy(resist, resist_hbm, sems.at[0])]
    copies[0].start()
    rows, columns = grad.shape
    chunks = CHUNKS if columns % (128 * CHUNKS) == 0 else 1
    high, low = split(merged[...])
    left = jnp.concatenate([high, low], axis=0)
    for at in range(chunks):
        part = pl.ds(at * (columns // chunks), columns // chunks)
        both = dot(left, table[0, :, part])
        product = both[:rows] + (both[rows:] + dot(high, table[1, :, part]))
        held = transmit[:, part]
        grad[:, part] = product * (1.0 - held * held)
        copy = pltpu.make_async_copy(grad.at[:, part], grad_hbm.at[:, part], sems.at[1 + at])
        copy.start()
        copies.append(copy)
    for copy in copies:
        copy.wait()


def shards(count, mask_params, target, kernel_spectra, kernel_weights):
    strip_rows, columns = mask_params.shape
    kernels, freq_rows, freq_cols = kernel_spectra.shape[1:]
    tables = make_tables(strip_rows, columns, freq_rows, freq_cols)
    names = list(tables)
    spectrum = (freq_rows, 2 * freq_cols)
    anywhere = pl.BlockSpec(memory_space=pl.ANY)
    out = jax.ShapeDtypeStruct((strip_rows, columns), jnp.float32)
    held = pltpu.VMEM((strip_rows, columns), jnp.float32)
    in_vmem = pl.BlockSpec(memory_space=pltpu.VMEM)
    merged = pltpu.VMEM((strip_rows, 2 * freq_cols), jnp.float32)
    last = pltpu.VMEM(tables["forward_back"].shape, jnp.bfloat16)
    results = pl.pallas_call(
        functools.partial(kernel, count, names),
        out_shape=(held, merged, held, last),
        in_specs=[pl.BlockSpec(memory_space=pltpu.SMEM)] + [anywhere] * (3 + len(names)),
        out_specs=(in_vmem,) * 4,
        scratch_shapes=[pltpu.VMEM(tables[n].shape, jnp.bfloat16) for n in names if n != "forward_back"]
        + [
            pltpu.VMEM((strip_rows, columns), jnp.float32),
            pltpu.VMEM((strip_rows, columns), jnp.int32),
            pltpu.VMEM(kernel_spectra.shape, jnp.float32),
            pltpu.VMEM((kernels // GROUP, 4 * freq_rows, GROUP * 2 * freq_cols), jnp.float32),
            pltpu.VMEM((2,) + spectrum, jnp.float32),
            pltpu.VMEM((2,) + spectrum, jnp.float32),
            pltpu.VMEM(spectrum, jnp.float32),
            pltpu.VMEM((2,) + spectrum, jnp.float32),
            pltpu.SemaphoreType.DMA((2 + 2 * CHUNKS + len(names),)),
            pltpu.SemaphoreType.DMA((4,)),
            pltpu.SemaphoreType.DMA((4,)),
        ],
        compiler_params=pltpu.CompilerParams(
            collective_id=0, has_side_effects=True, vmem_limit_bytes=56 * 1024 * 1024
        ),
        name="litho_step",
    )(kernel_weights, mask_params, target, kernel_spectra, *[jnp.asarray(t) for t in tables.values()])
    return pl.pallas_call(
        finish,
        out_shape=(out, out),
        in_specs=[in_vmem] * 4,
        out_specs=(anywhere, anywhere),
        scratch_shapes=[
            pltpu.VMEM((strip_rows, columns), jnp.float32),
            pltpu.SemaphoreType.DMA((1 + CHUNKS,)),
        ],
        compiler_params=pltpu.CompilerParams(vmem_limit_bytes=32 * 1024 * 1024),
        name="finish_gradient",
    )(*[pltpu.with_memory_space_constraint(x, pltpu.VMEM) for x in results])


def solution(mesh):
    rows = P(("parts", "tiles"), None)
    body = functools.partial(shards, mesh.shape["tiles"])
    return jax.shard_map(
        body, mesh=mesh, in_specs=(rows, rows, P(), P()), out_specs=(rows, rows), check_vma=False
    )
```
